128 devices in a mesh: dp: 8 (over x, z_hi), gallery: 16 (over z_lo, y, core).
Axes of the slice: x: 4, y: 4, z: 4 (z_hi: 2, z_lo: 2; z = z_hi * 2 + z_lo), core: 2. Of those that a mesh axis runs over, the one named last changes fastest.
Arguments:
- query_hidden: bfloat16 [1024, 32, 1536], P(('dp', 'gallery')), may hold values from -6 to 6
- document_states: bfloat16 [512, 768, 1536], P(('dp', 'gallery')), may hold values from -6 to 6
- projection: bfloat16 [1536, 128], replicated, may hold values from -0.15625 to 0.15625
- lengths: int32 [512], P(('dp', 'gallery')), may hold values from 192 to 768
- best_token: int32 [1024, 32, 64], P('dp', None, 'gallery'), may hold values from 0 to 767, as said below
Outputs:
- weight_grad: float32 [1536, 128], replicated
- query_grad: float32 [1024, 32, 128], P(('dp', 'gallery'))
The draws below stay inside these ranges and needn't reach their ends.
Inputs may be any that keep to these rules, and one draw needn't show every extreme that they name: best_token[b, i, p] is below the length of page p of query b's data group, that is below lengths[(b // 128) * 64 + p].
All inputs are finite; a program needn't handle non-finite values.
Results may differ from the reference program's by a relative error of at most 0.0041.
Values may be sent and summed in bfloat16 or wider, within the bound.
No kernel may reach another device: no remote copies, remote signals or barrier semaphores. Data moves between devices by JAX's collectives and lax.ppermute only.
A program may use at most 64 MiB of HBM per device.

```python
import jax
import jax.numpy as jnp
from jax import lax

HID = 1536
DIM = 128
QUESTION_LENGTH = 32
PLEN = 768
QUERIES_GROUP = 128
PAGES_GROUP = 64
QUERIES = 1024
PAGES = 512
N_DP = 8


def page_lengths(key):
    return jax.random.randint(key, (PAGES,), PLEN // 4, PLEN + 1).astype(jnp.int32)


def draw_lengths(key, part):
    return page_lengths(key)


def draw_best_token(key, part):
    boundaries = page_lengths(key)
    key = jax.random.fold_in(key, 7)
    raw_index = jax.random.randint(key, (QUERIES, QUESTION_LENGTH, PAGES_GROUP), 0, 1 << 20)
    group = jnp.arange(QUERIES) // QUERIES_GROUP
    page = group[:, None] * PAGES_GROUP + jnp.arange(PAGES_GROUP)[None, :]
    bound = boundaries[page]
    return (raw_index % bound[:, None, :]).astype(jnp.int32)


def block_levels(own_key, shape, cuts, least, largest):
    level, own = 1.0, jax.random.fold_in(own_key, 6)
    for axis_at, blocks in cuts:
        draws = jnp.exp(jax.random.uniform(jax.random.fold_in(own, axis_at), (blocks,), jnp.float32, least / len(cuts), largest / len(cuts)))
        level = level * jnp.repeat(draws, shape[axis_at] // blocks).reshape([-1 if axis == axis_at else 1 for axis in range(len(shape))])
    return level


def normal_values(own_key, dims, spread, most, split=(), kind=jnp.bfloat16):
    result = spread * jax.random.normal(own_key, dims, jnp.float32)
    if split:
        result = result * block_levels(own_key, dims, split, -0.22, 0.18)
    return jnp.clip(result, -most, most).astype(kind)


def setup_inputs(seed: int = 0) -> dict:
    key_list = jax.random.split(jax.random.key(seed), 6)
    return {
        "query_hidden": normal_values(key_list[0], (QUERIES, QUESTION_LENGTH, HID), 1.0, 6.0, ((0, 128),)),
        "document_states": normal_values(key_list[1], (PAGES, PLEN, HID), 1.0, 6.0, ((0, 128),)),
        "projection": normal_values(key_list[2], (HID, DIM), HID ** -0.5, 0.15625),
        "lengths": draw_lengths(jax.random.fold_in(key_list[5], 71), 0),
        "best_token": draw_best_token(jax.random.fold_in(key_list[5], 71), 0),
    }


epsilon = 1e-06
sharpness_divisor = 0.02

def unit_parts(hidden_rows, projection):
    raw = jnp.dot(hidden_rows, projection, preferred_element_type=jnp.float32)
    inverse = lax.rsqrt(lax.optimization_barrier(jnp.sum(raw * raw, axis=1, keepdims=True)) + epsilon)
    return (raw, inverse)

def unit_backward(grad_unit, raw, inverse):
    unit = raw * inverse
    return (grad_unit - unit * lax.optimization_barrier(jnp.sum(unit * grad_unit, axis=1, keepdims=True))) * inverse

def reference(query_hidden, document_states, projection, lengths, best_token):
    weight_grad = jnp.zeros((HID, DIM), jnp.float32)
    query_parts = []
    similarity_multiplier = 1.0 / (QUESTION_LENGTH * sharpness_divisor)
    for group in range(N_DP):
        query_rows = query_hidden[group * QUERIES_GROUP:(group + 1) * QUERIES_GROUP].reshape(-1, HID)
        query_raw, query_inverse = unit_parts(query_rows, projection)
        query_unit = (query_raw * query_inverse).astype(jnp.bfloat16)
        group_pages = document_states[group * PAGES_GROUP:(group + 1) * PAGES_GROUP]
        group_lengths = lengths[group * PAGES_GROUP:(group + 1) * PAGES_GROUP]
        batch_number = best_token[group * QUERIES_GROUP:(group + 1) * QUERIES_GROUP]

        def page_forward(inputs):
            page_hidden_rows, length = inputs
            raw, inverse = unit_parts(page_hidden_rows, projection)
            unit = (raw * inverse).astype(jnp.bfloat16)
            scores = jnp.dot(query_unit, unit.T, preferred_element_type=jnp.float32)
            valid = jnp.arange(PLEN)[None, :] < length
            best = lax.optimization_barrier(jnp.max(jnp.where(valid, scores, -jnp.inf), axis=1))
            return (best, unit)
        best, page_unit = lax.map(page_forward, (group_pages, group_lengths))
        score = lax.optimization_barrier(jnp.sum(best.T.reshape(QUERIES_GROUP, QUESTION_LENGTH, PAGES_GROUP), axis=1))
        expo = jnp.exp(score * similarity_multiplier)
        total = lax.optimization_barrier(jnp.sum(expo, axis=1, keepdims=True))
        target = jnp.arange(QUERIES_GROUP) * PAGES_GROUP // QUERIES_GROUP
        onehot = (target[:, None] == jnp.arange(PAGES_GROUP)[None, :]).astype(jnp.float32)
        score_grad = (expo / total - onehot) * similarity_multiplier
        chosen = page_unit[jnp.arange(PAGES_GROUP)[None, None, :], batch_number]
        query_grad = jnp.einsum('bipd,bp->bid', chosen.astype(jnp.float32), score_grad)
        query_parts.append(query_grad)
        query_dir = unit_backward(query_grad.reshape(-1, DIM), query_raw, query_inverse).astype(jnp.bfloat16)
        weight_grad = weight_grad + jnp.dot(query_rows.T, query_dir, preferred_element_type=jnp.float32)
        values = score_grad[:, None, :, None] * query_unit.reshape(QUERIES_GROUP, QUESTION_LENGTH, 1, DIM).astype(jnp.float32)

        def page_backward(carry, inputs):
            page_hidden_rows, page_index, page_values = inputs
            raw, inverse = unit_parts(page_hidden_rows, projection)
            normalized_derivative = jnp.zeros((PLEN, DIM), jnp.float32).at[page_index.reshape(-1)].add(page_values.reshape(-1, DIM))
            direction = unit_backward(normalized_derivative, raw, inverse).astype(jnp.bfloat16)
            return (carry + jnp.dot(page_hidden_rows.T, direction, preferred_element_type=jnp.float32), None)
        weight_grad, unused = lax.scan(page_backward, weight_grad, (group_pages, jnp.transpose(batch_number, (2, 0, 1)), jnp.transpose(values, (2, 0, 1, 3))))
    return (weight_grad, jnp.concatenate(query_parts, axis=0))
```

```python
import jax
import jax.numpy as jnp
from jax import lax
from jax.experimental import pallas as pl
from jax.experimental.pallas import tpu as pltpu
from jax.sharding import PartitionSpec as P

F32 = jnp.float32
BF16 = jnp.bfloat16
EPSILON = 1e-06
TEMPERATURE = 0.02
VMEM_LIMIT = 48 * 1024 * 1024

NT = (((1,), (1,)), ((), ()))
TN = (((0,), (0,)), ((), ()))


def inverse_norm(raw):
    return lax.rsqrt(jnp.sum(raw * raw, axis=1, keepdims=True) + EPSILON)


def unit_backward(grad_unit, raw, inverse):
    unit = raw * inverse
    return (grad_unit - unit * jnp.sum(unit * grad_unit, axis=1, keepdims=True)) * inverse


def lane_iota(shape):
    return lax.broadcasted_iota(jnp.int32, shape, len(shape) - 1)


def query_kernel(hidden_ref, weight_ref, raw_ref, unit_ref):
    raw = jnp.dot(hidden_ref[...], weight_ref[...], preferred_element_type=F32)
    raw_ref[...] = raw
    unit_ref[...] = (raw * inverse_norm(raw)).astype(BF16)


def page_kernel(length_ref, hidden_ref, weight_ref, index_ref, raw_ref, unit_ref, chosen_ref):
    page = pl.program_id(0)
    raw = jnp.dot(hidden_ref[0], weight_ref[...], preferred_element_type=F32)
    raw_ref[0] = raw
    unit = raw * inverse_norm(raw)
    slots = raw.shape[0]
    rows = lax.broadcasted_iota(jnp.int32, raw.shape, 0)
    unit_ref[0] = jnp.where(rows < length_ref[page], unit, unit[0:1]).astype(BF16)
    unit_t = unit.T.astype(BF16)
    positions = lax.broadcasted_iota(jnp.int32, (slots, 256), 0)

    def one_tile(tile, carry):
        at = pl.ds(pl.multiple_of(tile * 256, 256), 256)
        table = jnp.where(index_ref[0, :, at] == positions, 1.0, 0.0).astype(BF16)
        chosen_ref[0, :, at] = jnp.dot(unit_t, table, preferred_element_type=F32).astype(BF16)
        return carry

    lax.fori_loop(0, index_ref.shape[2] // 256, one_tile, 0)


def score_kernel(multiplier, rank_ref, query_ref, unit_ref, chosen_ref, expo_ref, send_ref, own_ref, target_ref, best, total):
    tile = pl.program_id(0)
    pages, slots, dim = unit_ref.shape
    queries = query_ref[0]
    for page in range(pages):
        top = None
        for start in range(0, slots, 256):
            scores = lax.dot_general(unit_ref[page, start:start + 256], queries, NT, preferred_element_type=F32)
            part = jnp.max(scores.reshape(32, 8, 256), axis=0)
            top = part if top is None else jnp.maximum(top, part)
        best[page:page + 1, :] = jnp.max(top, axis=0, keepdims=True)
    segment = jnp.where(
        lax.broadcasted_iota(jnp.int32, (256, 256), 0) // 32 == lane_iota((256, 256)) // 32, 1.0, 0.0
    ).astype(BF16)
    value = best[...]
    score = jnp.zeros_like(value)
    for _ in range(3):
        part = value.astype(BF16)
        score = score + jnp.dot(part, segment, preferred_element_type=F32)
        value = value - part.astype(F32)
    expo = jnp.exp(score * multiplier)
    mixed = jnp.zeros((dim, 256), F32)
    for page in range(pages):
        expo_ref[page, pl.ds(tile, 1), :] = expo[page:page + 1]
        mixed = mixed + expo[page:page + 1] * chosen_ref[page].astype(F32)
    mixed = mixed.T
    send_ref[tile, 0:256, :] = mixed.astype(BF16)
    row = jnp.sum(expo[0:pages], axis=0, keepdims=True)
    total[pl.ds(tile, 1), :] = jnp.where(lane_iota((1, 128)) % 32 < 16, row[:, :128], row[:, 128:])

    @pl.when(tile == rank_ref[0])
    def _():
        own_ref[...] = mixed
        picked = jnp.zeros((dim, 256), F32)
        for page in range(pages):
            picked = jnp.where(lane_iota((dim, 256)) // 64 == page, chosen_ref[page].astype(F32), picked)
        target_ref[...] = picked.T

    @pl.when(tile == pl.num_programs(0) - 1)
    def _():
        high = total[...].astype(BF16)
        low = (total[...] - high.astype(F32)).astype(BF16)
        for block in range(send_ref.shape[0]):
            send_ref[block, 256:272, :] = high
            send_ref[block, 272:288, :] = low


def gradient_kernel(multiplier, rank_ref, index_ref, expo_ref, received_ref, own_ref, target_ref, query_ref, page_raw_ref,
                    hidden_ref, query_raw_ref, query_hidden_ref, weight_ref, query_grad_ref, inverse_total, score_grad, accumulated):
    page = pl.program_id(0)
    rank = rank_ref[0]
    tiles = query_ref.shape[0]
    slots = hidden_ref.shape[1]

    @pl.when(page == 0)
    def _():
        total = jnp.zeros((tiles, 128), F32)
        for source in range(tiles):
            total = total + received_ref[source, 256:272, :].astype(F32) + received_ref[source, 272:288, :].astype(F32)
        inverse = 1.0 / total
        low_half = lane_iota((tiles, 128)) % 32 < 16
        inverse_total[:, 0:128] = jnp.where(low_half, inverse, pltpu.roll(inverse, 16, 1))
        inverse_total[:, 128:256] = jnp.where(low_half, pltpu.roll(inverse, 112, 1), inverse)
        summed = own_ref[...]
        for source in range(tiles):
            summed = summed + jnp.where(rank == source, 0.0, received_ref[source, 0:256, :].astype(F32))
        scale = jnp.broadcast_to(inverse_total[pl.ds(rank, 1), :], (128, 256)).T
        query_grad = (summed * scale - target_ref[...]) * multiplier
        query_grad_ref[...] = query_grad
        raw = query_raw_ref[...]
        direction = unit_backward(query_grad, raw, inverse_norm(raw)).astype(BF16)
        accumulated[...] = lax.dot_general(direction, query_hidden_ref[...], TN, preferred_element_type=F32)

    is_target = (lax.broadcasted_iota(jnp.int32, (tiles, 256), 0) == rank) & (lane_iota((tiles, 256)) // 64 == page)
    score_grad[...] = (expo_ref[0] * inverse_total[...] - jnp.where(is_target, 1.0, 0.0)) * multiplier
    positions = lax.broadcasted_iota(jnp.int32, (slots, 256), 0)

    def one_group(group, grad):
        for inner in range(4):
            tile = group * 4 + inner
            at = pl.ds(pl.multiple_of(tile * 256, 256), 256)
            table = jnp.where(index_ref[0, :, at] == positions, score_grad[pl.ds(tile, 1), :], 0.0).astype(BF16)
            grad = grad + jnp.dot(table, query_ref[tile], preferred_element_type=F32)
        return grad

    grad = lax.fori_loop(0, tiles // 4, one_group, jnp.zeros((slots, 128), F32))
    raw = page_raw_ref[0]
    direction = unit_backward(grad, raw, inverse_norm(raw)).astype(BF16)
    accumulated[...] += lax.dot_general(direction, hidden_ref[0], TN, preferred_element_type=F32)

    @pl.when(page == pl.num_programs(0) - 1)
    def _():
        weight_ref[...] = accumulated[...].T.astype(BF16)


def whole(shape):
    return pl.BlockSpec(shape, lambda i: (0,) * len(shape))


def per_device(query_hidden, document_states, projection, lengths, best_token):
    query_count, tokens, hidden_size = query_hidden.shape
    pages, slots, _ = document_states.shape
    dim = projection.shape[1]
    ranks = lax.axis_size("gallery")
    rank = lax.axis_index("gallery").astype(jnp.int32).reshape(1)
    rows = query_count * tokens
    all_rows = rows * ranks
    multiplier = 1.0 / (tokens * TEMPERATURE)
    smem = pl.BlockSpec(memory_space=pltpu.SMEM)
    params = pltpu.CompilerParams(vmem_limit_bytes=VMEM_LIMIT)
    query_rows = query_hidden.reshape(rows, hidden_size)

    query_raw, query_unit = pl.pallas_call(
        query_kernel,
        out_shape=(jax.ShapeDtypeStruct((rows, dim), F32), jax.ShapeDtypeStruct((rows, dim), BF16)),
        compiler_params=params,
        name="query_project",
    )(query_rows, projection)
    every_query = lax.all_to_all(jnp.broadcast_to(query_unit[None], (ranks, rows, dim)), "gallery", 0, 0, tiled=True)

    index = jnp.transpose(best_token, (2, 0, 1)).reshape(pages, 1, all_rows)
    page_raw, page_unit, chosen = pl.pallas_call(
        page_kernel,
        grid=(pages,),
        in_specs=[
            smem,
            pl.BlockSpec((1, slots, hidden_size), lambda i: (i, 0, 0)),
            whole((hidden_size, dim)),
            pl.BlockSpec((1, 1, all_rows), lambda i: (i, 0, 0)),
        ],
        out_specs=[
            pl.BlockSpec((1, slots, dim), lambda i: (i, 0, 0)),
            pl.BlockSpec((1, slots, dim), lambda i: (i, 0, 0)),
            pl.BlockSpec((1, dim, all_rows), lambda i: (i, 0, 0)),
        ],
        out_shape=(
            jax.ShapeDtypeStruct((pages, slots, dim), F32),
            jax.ShapeDtypeStruct((pages, slots, dim), BF16),
            jax.ShapeDtypeStruct((pages, dim, all_rows), BF16),
        ),
        compiler_params=params,
        cost_estimate=pl.CostEstimate(flops=2 * pages * slots * dim * (hidden_size + all_rows), bytes_accessed=16 << 20, transcendentals=0),
        name="page_project",
    )(lengths, document_states, projection, index)

    expo, send, own, target = pl.pallas_call(
        lambda *refs: score_kernel(multiplier, *refs),
        grid=(ranks,),
        in_specs=[
            smem,
            pl.BlockSpec((1, rows, dim), lambda i: (i, 0, 0)),
            whole((pages, slots, dim)),
            pl.BlockSpec((pages, dim, rows), lambda i: (0, 0, i)),
        ],
        out_specs=[whole((pages, ranks, rows)), whole((ranks, rows + 32, dim)), whole((rows, dim)), whole((rows, dim))],
        out_shape=(
            jax.ShapeDtypeStruct((pages, ranks, rows), F32),
            jax.ShapeDtypeStruct((ranks, rows + 32, dim), BF16),
            jax.ShapeDtypeStruct((rows, dim), F32),
            jax.ShapeDtypeStruct((rows, dim), F32),
        ),
        scratch_shapes=[pltpu.VMEM((8, rows), F32), pltpu.VMEM((ranks, 128), F32)],
        compiler_params=params,
        cost_estimate=pl.CostEstimate(flops=2 * pages * slots * dim * all_rows, bytes_accessed=8 << 20, transcendentals=0),
        name="scores",
    )(rank, every_query, page_unit, chosen)
    received = lax.all_to_all(send, "gallery", 0, 0, tiled=True)

    weight_part, query_grad = pl.pallas_call(
        lambda *refs: gradient_kernel(multiplier, *refs),
        grid=(pages,),
        in_specs=[
            smem,
            pl.BlockSpec((1, 1, all_rows), lambda i: (i, 0, 0)),
            pl.BlockSpec((1, ranks, rows), lambda i: (i, 0, 0)),
            whole((ranks, rows + 32, dim)),
            whole((rows, dim)),
            whole((rows, dim)),
            whole((ranks, rows, dim)),
            pl.BlockSpec((1, slots, dim), lambda i: (i, 0, 0)),
            pl.BlockSpec((1, slots, hidden_size), lambda i: (i, 0, 0)),
            whole((rows, dim)),
            whole((rows, hidden_size)),
        ],
        out_specs=[whole((hidden_size, dim)), whole((rows, dim))],
        out_shape=(jax.ShapeDtypeStruct((hidden_size, dim), BF16), jax.ShapeDtypeStruct((rows, dim), F32)),
        scratch_shapes=[pltpu.VMEM((ranks, rows), F32), pltpu.VMEM((ranks, rows), F32), pltpu.VMEM((dim, hidden_size), F32)],
        compiler_params=params,
        cost_estimate=pl.CostEstimate(flops=2 * pages * slots * dim * (hidden_size + all_rows), bytes_accessed=16 << 20, transcendentals=0),
        name="gradients",
    )(rank, index, expo, received, own, target, every_query, page_raw, document_states, query_raw, query_rows)

    devices = ranks * lax.axis_size("dp")
    chunk = hidden_size // devices
    parts = lax.all_to_all(weight_part.reshape(devices, chunk, dim), ("dp", "gallery"), 0, 0, tiled=True)
    mine = jnp.sum(parts.astype(F32), axis=0).astype(BF16)
    shared = lax.all_to_all(jnp.broadcast_to(mine[None], (devices, chunk, dim)), ("dp", "gallery"), 0, 0, tiled=True)
    weight_grad = shared.reshape(hidden_size, dim).astype(F32)
    return (weight_grad, query_grad.reshape(query_count, tokens, dim))


def solution(mesh):
    return jax.shard_map(
        per_device,
        mesh=mesh,
        in_specs=(
            P(("dp", "gallery"), None, None),
            P(("dp", "gallery"), None, None),
            P(),
            P(("dp", "gallery")),
            P("dp", None, "gallery"),
        ),
        out_specs=(P(), P(("dp", "gallery"), None, None)),
        check_vma=False,
    )
```

```python
import jax
import jax.numpy as jnp
from jax import lax
from jax.experimental import pallas as pl
from jax.experimental.pallas import tpu as pltpu
from jax.sharding import Mesh, PartitionSpec as P

F32 = jnp.float32
BF16 = jnp.bfloat16
EPSILON = 1e-06
TEMPERATURE = 0.02
MIB = 1024 * 1024

NT = (((1,), (1,)), ((), ()))
TN = (((0,), (0,)), ((), ()))


def inverse_norm(raw, axis):
    value = jnp.sum(raw * raw, axis=axis, keepdims=True) + EPSILON
    guess = lax.rsqrt(value)
    return guess * (1.5 - 0.5 * value * guess * guess)


def unit_backward(grad_unit, raw):
    inverse = inverse_norm(raw, 0)
    unit = raw * inverse
    return (grad_unit - unit * jnp.sum(unit * grad_unit, axis=0, keepdims=True)) * inverse


def iota(shape, axis):
    return lax.broadcasted_iota(jnp.int32, shape, axis)


def one_hot(index, rows):
    return jnp.where(iota((rows, index.shape[1]), 0) == index, 1.0, 0.0).astype(BF16)


def query_kernel(hidden_ref, weight_ref, raw_ref, send_ref):
    raw = jnp.dot(hidden_ref[...], weight_ref[...], preferred_element_type=F32).T
    raw_ref[...] = raw
    unit = (raw * inverse_norm(raw, 0)).astype(BF16)
    for block in range(send_ref.shape[0]):
        send_ref[block] = unit


def page_kernel(length_ref, hidden_ref, weight_ref, index_ref, raw_ref, unit_ref, chosen_ref):
    page = pl.program_id(0)
    raw = jnp.dot(hidden_ref[0], weight_ref[...], preferred_element_type=F32)
    raw_t = raw.T
    raw_ref[0] = raw_t
    unit = raw_t * inverse_norm(raw_t, 0)
    slots = unit.shape[1]
    unit_ref[0] = jnp.where(iota(unit.shape, 1) < length_ref[page], unit, unit[:, 0:1]).T.astype(BF16)
    unit = unit.astype(BF16)
    parts = slots // 256
    table = jnp.concatenate([unit[:, part * 256:(part + 1) * 256] for part in range(parts)], axis=0)

    def one_tile(tile, carry):
        index = index_ref[0, pl.ds(tile, 1), :]
        found = jnp.dot(table, one_hot(index & 255, 256), preferred_element_type=F32)
        which = index >> 8
        chosen = found[0:128]
        for part in range(1, parts):
            chosen = jnp.where(which == part, found[part * 128:(part + 1) * 128], chosen)
        chosen_ref[0, tile] = chosen.astype(BF16)
        return carry

    lax.fori_loop(0, index_ref.shape[1], one_tile, 0, unroll=4)


def best_scores(queries, unit_ref, out, row):
    for page in range(unit_ref.shape[0]):
        scores = jnp.dot(unit_ref[page], queries, preferred_element_type=F32)
        top = jnp.max(scores.reshape(-1, 8, scores.shape[1]), axis=0)
        out[page, pl.ds(row, 1), :] = jnp.max(top, axis=0, keepdims=True)


def near_kernel(query_ref, unit_ref, best_ref):
    def one_tile(tile, carry):
        best_scores(query_ref[tile], unit_ref, best_ref, tile)
        return carry

    lax.fori_loop(0, query_ref.shape[0], one_tile, 0, unroll=2)


def far_kernel(multiplier, place_ref, query_ref, unit_ref, near_ref, chosen_ref, expo_ref, keep_ref, total_ref, pair_ref, target_ref, best):
    core, chip = place_ref[0], place_ref[1]
    pages, chips = near_ref.shape[:2]
    dim, lanes = query_ref.shape[1:]
    near = pl.multiple_of(core * chips, chips)
    far = pl.multiple_of((1 - core) * chips, chips)
    for page in range(pages):
        best[page, pl.ds(near, chips), :] = near_ref[page]

    def one_tile(tile, carry):
        best_scores(query_ref[tile], unit_ref, best, far + tile)
        return carry

    lax.fori_loop(0, chips, one_tile, 0, unroll=2)

    segment = jnp.where(iota((lanes, lanes), 0) // 32 == iota((lanes, lanes), 1) // 32, 1.0, 0.0).astype(BF16)
    value = best[...].reshape(pages * 2 * chips, lanes)
    score = jnp.zeros_like(value)
    for _ in range(3):
        part = value.astype(BF16)
        score = score + jnp.dot(part, segment, preferred_element_type=F32)
        value = value - part.astype(F32)
    expo = jnp.exp(score * multiplier).reshape(pages, 2 * chips, lanes)
    expo_ref[...] = expo
    total = jnp.sum(expo, axis=0)
    total = jnp.where(iota((2 * chips, 128), 1) % 32 < 16, total[:, :128], total[:, 128:])
    total_ref[...] = total
    high = total.astype(BF16)
    low = (total - high.astype(F32)).astype(BF16)

    def mixed(tile):
        result = jnp.zeros((dim, lanes), F32)
        for page in range(pages):
            result = result + expo_ref[page, pl.ds(tile, 1), :] * chosen_ref[page, tile].astype(F32)
        return result

    def one_mix(tile, carry):
        pair_ref[tile, 0:dim, :] = mixed(far + tile).astype(BF16)
        pair_ref[tile, dim:dim + 16, 0:128] = high
        pair_ref[tile, dim:dim + 16, 128:256] = low
        keep_ref[tile] = mixed(near + tile)
        return carry

    lax.fori_loop(0, chips, one_mix, 0, unroll=2)
    picked = jnp.zeros((dim, lanes), F32)
    for page in range(pages):
        picked = jnp.where(iota((dim, lanes), 1) // 64 == page, chosen_ref[page, near + chip].astype(F32), picked)
    target_ref[...] = picked


def add_kernel(place_ref, keep_ref, total_ref, pair_ref, send_ref, own_ref):
    chips, dim, _ = keep_ref.shape
    total = total_ref[...] + (pair_ref[0, dim:dim + 16, 0:128].astype(F32) + pair_ref[0, dim:dim + 16, 128:256].astype(F32))
    high = total.astype(BF16)
    low = (total - high.astype(F32)).astype(BF16)
    for tile in range(chips):
        send_ref[tile, 0:dim, :] = (keep_ref[tile] + pair_ref[tile, 0:dim, :].astype(F32)).astype(BF16)
        send_ref[tile, dim:dim + 16, 0:128] = high
        send_ref[tile, dim:dim + 16, 128:256] = low
    chip = place_ref[1]
    own_ref[...] = keep_ref[chip] + pair_ref[chip, 0:dim, :].astype(F32)


def gradient_kernel(multiplier, place_ref, index_ref, expo_ref, received_ref, own_ref, target_ref, near_ref, far_ref, page_raw_ref,
                    hidden_ref, query_raw_ref, query_hidden_ref, weight_ref, query_grad_ref, inverse_total, score_grad, query_scratch, accumulated):
    page = pl.program_id(0)
    core, chip = place_ref[0], place_ref[1]
    chips, dim, lanes = near_ref.shape
    tiles = 2 * chips
    mine = core * chips + chip
    slots = hidden_ref.shape[1]
    parts = slots // 256

    @pl.when(page == 0)
    def _():
        total = jnp.zeros((tiles, 128), F32)
        for source in range(chips):
            total = total + received_ref[source, dim:dim + 16, 0:128].astype(F32) + received_ref[source, dim:dim + 16, 128:256].astype(F32)
        inverse = 1.0 / total
        first = iota((tiles, 128), 1) % 32 < 16
        inverse_total[:, 0:128] = jnp.where(first, inverse, pltpu.roll(inverse, 16, 1))
        inverse_total[:, 128:256] = jnp.where(first, pltpu.roll(inverse, 112, 1), inverse)
        summed = own_ref[...]
        for source in range(chips):
            summed = summed + jnp.where(chip == source, 0.0, received_ref[source, 0:dim, :].astype(F32))
        query_grad = (summed * inverse_total[pl.ds(mine, 1), :] - target_ref[...]) * multiplier
        query_grad_ref[...] = query_grad.T
        direction = unit_backward(query_grad, query_raw_ref[...]).astype(BF16)
        accumulated[...] = jnp.dot(direction, query_hidden_ref[...], preferred_element_type=F32)
        query_scratch[pl.ds(core * chips, chips)] = near_ref[...]
        query_scratch[pl.ds((1 - core) * chips, chips)] = far_ref[...]

    is_target = (iota((tiles, lanes), 0) == mine) & (iota((tiles, lanes), 1) // 64 == page)
    score_grad[...] = (expo_ref[0] * inverse_total[...] - jnp.where(is_target, 1.0, 0.0)) * multiplier

    def one_group(group, grad):
        lefts, tables = [], []
        for inner in range(4):
            tile = group * 4 + inner
            index = index_ref[0, pl.ds(tile, 1), :]
            weighted = query_scratch[tile].astype(F32) * score_grad[pl.ds(tile, 1), :]
            which = index >> 8
            lefts.append(jnp.concatenate([jnp.where(which == part, weighted, 0.0).astype(BF16) for part in range(parts)], axis=0))
            tables.append(one_hot(index & 255, 256))
        left = jnp.concatenate(lefts, axis=1)
        table = jnp.concatenate(tables, axis=1)
        return grad + lax.dot_general(left, table, NT, preferred_element_type=F32)

    grad = lax.fori_loop(0, tiles // 4, one_group, jnp.zeros((parts * dim, 256), F32))
    grad = jnp.concatenate([grad[part * dim:(part + 1) * dim] for part in range(parts)], axis=1)
    direction = unit_backward(grad, page_raw_ref[0]).astype(BF16)
    accumulated[...] += jnp.dot(direction, hidden_ref[0], preferred_element_type=F32)

    @pl.when(page == pl.num_programs(0) - 1)
    def _():
        weight_ref[...] = accumulated[...].T.astype(BF16)


def whole(shape):
    return pl.BlockSpec(shape, lambda *i: (0,) * len(shape))


def shape(dims, kind):
    return jax.ShapeDtypeStruct(dims, kind)


def vmem(mib):
    return pltpu.CompilerParams(vmem_limit_bytes=mib * MIB)


def cost(flops, read):
    return pl.CostEstimate(flops=flops, bytes_accessed=read, transcendentals=0)


def swap_cores(value):
    return lax.ppermute(value, "core", [(0, 1), (1, 0)])


def per_device(query_hidden, document_states, projection, lengths, best_token):
    query_count, tokens, hidden_size = query_hidden.shape
    pages, slots, _ = document_states.shape
    dim = projection.shape[1]
    chips, cores = lax.axis_size("chip"), lax.axis_size("core")
    tiles = chips * cores
    rows = query_count * tokens
    multiplier = 1.0 / (tokens * TEMPERATURE)
    smem = pl.BlockSpec(memory_space=pltpu.SMEM)
    place = jnp.stack([lax.axis_index("core"), lax.axis_index("chip")]).astype(jnp.int32)
    query_rows = query_hidden.reshape(rows, hidden_size)

    query_raw, query_send = pl.pallas_call(
        query_kernel,
        out_shape=(shape((dim, rows), F32), shape((chips, dim, rows), BF16)),
        compiler_params=vmem(8),
        name="query_project",
    )(query_rows, projection)
    near = lax.all_to_all(query_send, "chip", 0, 0, tiled=True)

    index = jnp.transpose(best_token.reshape(chips, cores, query_count, tokens, pages), (4, 1, 0, 2, 3)).reshape(pages, tiles, rows)
    page_raw, page_unit, chosen = pl.pallas_call(
        page_kernel,
        grid=(pages,),
        in_specs=[
            smem,
            pl.BlockSpec((1, slots, hidden_size), lambda i: (i, 0, 0)),
            whole((hidden_size, dim)),
            pl.BlockSpec((1, tiles, rows), lambda i: (i, 0, 0)),
        ],
        out_specs=[
            pl.BlockSpec((1, dim, slots), lambda i: (i, 0, 0)),
            pl.BlockSpec((1, slots, dim), lambda i: (i, 0, 0)),
            pl.BlockSpec((1, tiles, dim, rows), lambda i: (i, 0, 0, 0)),
        ],
        out_shape=(shape((pages, dim, slots), F32), shape((pages, slots, dim), BF16), shape((pages, tiles, dim, rows), BF16)),
        compiler_params=vmem(24),
        cost_estimate=cost(2 * pages * slots * dim * (hidden_size + tiles * rows), 16 * MIB),
        name="page_project",
    )(lengths, document_states, projection, index)

    far = swap_cores(near)
    near_best = pl.pallas_call(
        near_kernel,
        out_shape=shape((pages, chips, rows), F32),
        compiler_params=vmem(16),
        cost_estimate=cost(pages * slots * dim * tiles * rows, 2 * MIB),
        name="near_scores",
    )(near, page_unit)
    expo, keep, total, pair, target = pl.pallas_call(
        lambda *refs: far_kernel(multiplier, *refs),
        in_specs=[smem] + [pl.BlockSpec(memory_space=pltpu.VMEM)] * 4,
        out_shape=(
            shape((pages, tiles, rows), F32),
            shape((chips, dim, rows), F32),
            shape((tiles, 128), F32),
            shape((chips, dim + 16, rows), BF16),
            shape((dim, rows), F32),
        ),
        scratch_shapes=[pltpu.VMEM((pages, tiles, rows), F32)],
        compiler_params=vmem(24),
        cost_estimate=cost(pages * slots * dim * tiles * rows, 8 * MIB),
        name="far_scores",
    )(place, far, page_unit, near_best, chosen)
    send, own = pl.pallas_call(
        add_kernel,
        in_specs=[smem] + [pl.BlockSpec(memory_space=pltpu.VMEM)] * 3,
        out_shape=(shape((chips, dim + 16, rows), BF16), shape((dim, rows), F32)),
        compiler_params=vmem(8),
        name="add_pair",
    )(place, keep, total, swap_cores(pair))
    received = lax.all_to_all(send, "chip", 0, 0, tiled=True)

    weight_part, query_grad = pl.pallas_call(
        lambda *refs: gradient_kernel(multiplier, *refs),
        grid=(pages,),
        in_specs=[
            smem,
            pl.BlockSpec((1, tiles, rows), lambda i: (i, 0, 0)),
            pl.BlockSpec((1, tiles, rows), lambda i: (i, 0, 0)),
            whole((chips, dim + 16, rows)),
            whole((dim, rows)),
            whole((dim, rows)),
            whole((chips, dim, rows)),
            whole((chips, dim, rows)),
            pl.BlockSpec((1, dim, slots), lambda i: (i, 0, 0)),
            pl.BlockSpec((1, slots, hidden_size), lambda i: (i, 0, 0)),
            whole((dim, rows)),
            whole((rows, hidden_size)),
        ],
        out_specs=[whole((hidden_size, dim)), whole((rows, dim))],
        out_shape=(shape((hidden_size, dim), BF16), shape((rows, dim), F32)),
        scratch_shapes=[
            pltpu.VMEM((tiles, rows), F32),
            pltpu.VMEM((tiles, rows), F32),
            pltpu.VMEM((tiles, dim, rows), BF16),
            pltpu.VMEM((dim, hidden_size), F32),
        ],
        compiler_params=vmem(32),
        cost_estimate=cost(2 * pages * slots * dim * (hidden_size + tiles * rows), 16 * MIB),
        name="gradients",
    )(place, index, expo, received, own, target, near, far, page_raw, document_states, query_raw, query_rows)

    everyone = ("dp", "chip", "core")
    devices = lax.axis_size(everyone)
    chunk = hidden_size // devices
    terms = lax.all_to_all(weight_part.reshape(devices, chunk, dim), everyone, 0, 0, tiled=True)
    mine = jnp.sum(terms.astype(F32), axis=0).astype(BF16)
    shared = lax.all_to_all(jnp.broadcast_to(mine[None], (devices, chunk, dim)), everyone, 0, 0, tiled=True)
    weight_grad = shared.reshape(hidden_size, dim).astype(F32)
    return (weight_grad, query_grad.reshape(query_count, tokens, dim))


def solution(mesh):
    groups, gallery = mesh.devices.shape
    levels = Mesh(mesh.devices.reshape(groups, gallery // 2, 2), ("dp", "chip", "core"))
    every = ("dp", "chip", "core")
    return jax.shard_map(
        per_device,
        mesh=levels,
        in_specs=(P(every, None, None), P(every, None, None), P(), P(every), P("dp", None, ("chip", "core"))),
        out_specs=(P(), P(every, None, None)),
        check_vma=False,
    )
```

```python
import jax
import jax.numpy as jnp
from jax import lax
from jax.experimental import pallas as pl
from jax.experimental.pallas import tpu as pltpu
from jax.sharding import Mesh, PartitionSpec as P

F32 = jnp.float32
BF16 = jnp.bfloat16
EPSILON = 1e-06
TEMPERATURE = 0.02
MIB = 1024 * 1024
QUERY_MIB, PAGE_MIB, GRADIENT_MIB = 60, 50, 50

NT = (((1,), (1,)), ((), ()))
TN = (((0,), (0,)), ((), ()))


def inverse_norm(raw, axis):
    value = jnp.sum(raw * raw, axis=axis, keepdims=True) + EPSILON
    guess = lax.rsqrt(value)
    return guess * (1.5 - 0.5 * value * guess * guess)


def unit_backward(grad_unit, raw):
    inverse = inverse_norm(raw, 0)
    unit = raw * inverse
    return (grad_unit - unit * jnp.sum(unit * grad_unit, axis=0, keepdims=True)) * inverse


def iota(shape, axis):
    return lax.broadcasted_iota(jnp.int32, shape, axis)


def one_hot(low):
    index = low.astype(F32).astype(BF16)
    positions = iota((256, low.shape[1]), 0).astype(F32).astype(BF16)
    return jnp.where(positions == index, jnp.ones((), BF16), jnp.zeros((), BF16))


def query_kernel(hidden_any, weight_any, raw_ref, send_ref, hidden, weight, arrived):
    copies = [
        pltpu.make_async_copy(weight_any, weight, arrived.at[0]),
        pltpu.make_async_copy(hidden_any, hidden, arrived.at[1]),
    ]
    for copy in copies:
        copy.start()
    for copy in copies:
        copy.wait()
    raw = jnp.dot(hidden[...], weight[...], preferred_element_type=F32).T
    raw_ref[...] = raw
    unit = (raw * inverse_norm(raw, 0)).astype(BF16)
    for block in range(send_ref.shape[0]):
        send_ref[block] = unit


def page_kernel(length_ref, hidden_ref, weight_ref, index_ref, raw_ref, unit_ref, chosen_ref):
    page = pl.program_id(0)
    raw = jnp.dot(hidden_ref[0], weight_ref[...], preferred_element_type=F32)
    raw_t = raw.T
    raw_ref[0] = raw_t
    unit = raw_t * inverse_norm(raw_t, 0)
    slots = unit.shape[1]
    unit_ref[0] = jnp.where(iota(unit.shape, 1) < length_ref[page], unit, unit[:, 0:1]).T.astype(BF16)
    unit = unit.astype(BF16)
    parts = slots // 256
    table = jnp.concatenate([unit[:, part * 256:(part + 1) * 256] for part in range(parts)], axis=0)

    def one_tile(tile, carry):
        index = index_ref[0, pl.ds(tile, 1), :]
        found = jnp.dot(table, one_hot(index & 255), preferred_element_type=F32)
        which = index >> 8
        chosen = found[0:128]
        for part in range(1, parts):
            chosen = jnp.where(which == part, found[part * 128:(part + 1) * 128], chosen)
        chosen_ref[0, tile] = chosen.astype(BF16)
        return carry

    lax.fori_loop(0, index_ref.shape[1], one_tile, 0, unroll=8)


def best_scores(queries, unit_ref, out, row):
    for page in range(unit_ref.shape[0]):
        scores = jnp.dot(unit_ref[page], queries, preferred_element_type=F32)
        top = jnp.max(scores.reshape(-1, 8, scores.shape[1]), axis=0)
        out[page, pl.ds(row, 1), :] = jnp.max(top, axis=0, keepdims=True)


def near_kernel(query_ref, unit_ref, best_ref):
    def one_tile(tile, carry):
        best_scores(query_ref[tile], unit_ref, best_ref, tile)
        return carry

    lax.fori_loop(0, query_ref.shape[0], one_tile, 0, unroll=2)


def far_kernel(multiplier, place_ref, query_ref, unit_ref, near_ref, chosen_ref, expo_ref, keep_ref, total_ref, pair_ref, target_ref, best):
    core, chip = place_ref[0], place_ref[1]
    pages, chips = near_ref.shape[:2]
    dim, lanes = query_ref.shape[1:]
    near = pl.multiple_of(core * chips, chips)
    far = pl.multiple_of((1 - core) * chips, chips)
    for page in range(pages):
        best[page, pl.ds(near, chips), :] = near_ref[page]

    def one_tile(tile, carry):
        best_scores(query_ref[tile], unit_ref, best, far + tile)
        return carry

    lax.fori_loop(0, chips, one_tile, 0, unroll=2)

    segment = jnp.where(iota((lanes, lanes), 0) // 32 == iota((lanes, lanes), 1) // 32, 1.0, 0.0).astype(BF16)
    value = best[...].reshape(pages * 2 * chips, lanes)
    score = jnp.zeros_like(value)
    for _ in range(3):
        part = value.astype(BF16)
        score = score + jnp.dot(part, segment, preferred_element_type=F32)
        value = value - part.astype(F32)
    expo = jnp.exp(score * multiplier).reshape(pages, 2 * chips, lanes)
    expo_ref[...] = expo
    total = jnp.sum(expo, axis=0)
    total = jnp.where(iota((2 * chips, 128), 1) % 32 < 16, total[:, :128], total[:, 128:])
    total_ref[...] = total
    high = total.astype(BF16)
    low = (total - high.astype(F32)).astype(BF16)

    def mixed(tile):
        result = jnp.zeros((dim, lanes), F32)
        for page in range(pages):
            result = result + expo_ref[page, pl.ds(tile, 1), :] * chosen_ref[page, tile].astype(F32)
        return result

    def one_mix(tile, carry):
        pair_ref[tile, 0:dim, :] = mixed(far + tile).astype(BF16)
        pair_ref[tile, dim:dim + 16, 0:128] = high
        pair_ref[tile, dim:dim + 16, 128:256] = low
        keep_ref[tile] = mixed(near + tile)
        return carry

    lax.fori_loop(0, chips, one_mix, 0, unroll=2)
    picked = jnp.zeros((dim, lanes), F32)
    for page in range(pages):
        picked = jnp.where(iota((dim, lanes), 1) // 64 == page, chosen_ref[page, near + chip].astype(F32), picked)
    target_ref[...] = picked


def add_kernel(place_ref, keep_ref, total_ref, pair_ref, send_ref, own_ref):
    chips, dim, _ = keep_ref.shape
    total = total_ref[...] + (pair_ref[0, dim:dim + 16, 0:128].astype(F32) + pair_ref[0, dim:dim + 16, 128:256].astype(F32))
    high = total.astype(BF16)
    low = (total - high.astype(F32)).astype(BF16)
    for tile in range(chips):
        send_ref[tile, 0:dim, :] = (keep_ref[tile] + pair_ref[tile, 0:dim, :].astype(F32)).astype(BF16)
        send_ref[tile, dim:dim + 16, 0:128] = high
        send_ref[tile, dim:dim + 16, 128:256] = low
    chip = place_ref[1]
    own_ref[...] = keep_ref[chip] + pair_ref[chip, 0:dim, :].astype(F32)


def gradient_kernel(multiplier, place_ref, index_ref, expo_ref, received_ref, own_ref, target_ref, near_ref, far_ref, page_raw_ref,
                    hidden_any, query_raw_ref, query_hidden_any, weight_ref, query_grad_ref, inverse_total, score_grad, summed_grad,
                    accumulated, hidden, query_hidden, arrived):
    page = pl.program_id(0)
    core, chip = place_ref[0], place_ref[1]
    chips, dim, lanes = near_ref.shape
    tiles = 2 * chips
    mine = core * chips + chip
    pages, slots, _ = hidden.shape
    parts = slots // 256
    query_copy = pltpu.make_async_copy(query_hidden_any, query_hidden, arrived.at[pages])

    def page_copy(which):
        return pltpu.make_async_copy(hidden_any.at[which], hidden.at[which], arrived.at[which])

    @pl.when(page == 0)
    def _():
        query_copy.start()
        for which in range(pages):
            page_copy(which).start()
        total = jnp.zeros((tiles, 128), F32)
        for source in range(chips):
            total = total + received_ref[source, dim:dim + 16, 0:128].astype(F32) + received_ref[source, dim:dim + 16, 128:256].astype(F32)
        inverse = 1.0 / total
        first = iota((tiles, 128), 1) % 32 < 16
        inverse_total[:, 0:128] = jnp.where(first, inverse, pltpu.roll(inverse, 16, 1))
        inverse_total[:, 128:256] = jnp.where(first, pltpu.roll(inverse, 112, 1), inverse)
        summed = own_ref[...]
        for source in range(chips):
            summed = summed + jnp.where(chip == source, 0.0, received_ref[source, 0:dim, :].astype(F32))
        query_grad = (summed * inverse_total[pl.ds(mine, 1), :] - target_ref[...]) * multiplier
        query_grad_ref[...] = query_grad.T
        direction = unit_backward(query_grad, query_raw_ref[...]).astype(BF16)
        query_copy.wait()
        accumulated[...] = jnp.dot(direction, query_hidden[...], preferred_element_type=F32)

    is_target = (iota((tiles, lanes), 0) == mine) & (iota((tiles, lanes), 1) // 64 == page)
    score_grad[...] = (expo_ref[0] * inverse_total[...] - jnp.where(is_target, 1.0, 0.0)) * multiplier

    for side, queries_ref in ((core, near_ref), (1 - core, far_ref)):
        for chip_of in range(chips):
            tile = side * chips + chip_of
            index = index_ref[0, pl.ds(tile, 1), :]
            weighted = queries_ref[chip_of].astype(F32) * score_grad[pl.ds(tile, 1), :]
            which = index >> 8
            left = jnp.concatenate([jnp.where(which == part, weighted, 0.0).astype(BF16) for part in range(parts)], axis=0)
            term = lax.dot_general(left, one_hot(index & 255), NT, preferred_element_type=F32)
            if queries_ref is near_ref and chip_of == 0:
                summed_grad[...] = term
            else:
                summed_grad[...] += term
    grad = jnp.concatenate([summed_grad[part * dim:(part + 1) * dim] for part in range(parts)], axis=1)
    direction = unit_backward(grad, page_raw_ref[0]).astype(BF16)
    page_copy(page).wait()
    accumulated[...] += jnp.dot(direction, hidden[page], preferred_element_type=F32)

    @pl.when(page == pl.num_programs(0) - 1)
    def _():
        weight_ref[...] = accumulated[...].T.astype(BF16)


def whole(shape):
    return pl.BlockSpec(shape, lambda *i: (0,) * len(shape))


def shape(dims, kind):
    return jax.ShapeDtypeStruct(dims, kind)


def vmem(mib):
    return pltpu.CompilerParams(vmem_limit_bytes=mib * MIB)


def cost(flops, read):
    return pl.CostEstimate(flops=flops, bytes_accessed=read, transcendentals=0)


def swap_cores(value):
    return lax.ppermute(value, "core", [(0, 1), (1, 0)])


def per_device(query_hidden, document_states, projection, lengths, best_token):
    query_count, tokens, hidden_size = query_hidden.shape
    pages, slots, _ = document_states.shape
    dim = projection.shape[1]
    chips, cores = lax.axis_size("chip"), lax.axis_size("core")
    tiles = chips * cores
    rows = query_count * tokens
    multiplier = 1.0 / (tokens * TEMPERATURE)
    smem = pl.BlockSpec(memory_space=pltpu.SMEM)
    place = jnp.stack([lax.axis_index("core"), lax.axis_index("chip")]).astype(jnp.int32)
    query_rows = query_hidden.reshape(rows, hidden_size)

    query_raw, query_send = pl.pallas_call(
        query_kernel,
        in_specs=[pl.BlockSpec(memory_space=pl.ANY)] * 2,
        out_shape=(shape((dim, rows), F32), shape((chips, dim, rows), BF16)),
        scratch_shapes=[pltpu.VMEM((rows, hidden_size), BF16), pltpu.VMEM((hidden_size, dim), BF16), pltpu.SemaphoreType.DMA((2,))],
        compiler_params=vmem(QUERY_MIB),
        name="query_project",
    )(query_rows, projection)
    near = lax.all_to_all(query_send, "chip", 0, 0, tiled=True)

    index = jnp.transpose(best_token.reshape(chips, cores, query_count, tokens, pages), (4, 1, 0, 2, 3)).reshape(pages, tiles, rows)
    page_raw, page_unit, chosen = pl.pallas_call(
        page_kernel,
        grid=(pages,),
        in_specs=[
            smem,
            pl.BlockSpec((1, slots, hidden_size), lambda i: (i, 0, 0)),
            whole((hidden_size, dim)),
            pl.BlockSpec((1, tiles, rows), lambda i: (i, 0, 0)),
        ],
        out_specs=[
            pl.BlockSpec((1, dim, slots), lambda i: (i, 0, 0)),
            pl.BlockSpec((1, slots, dim), lambda i: (i, 0, 0)),
            pl.BlockSpec((1, tiles, dim, rows), lambda i: (i, 0, 0, 0)),
        ],
        out_shape=(shape((pages, dim, slots), F32), shape((pages, slots, dim), BF16), shape((pages, tiles, dim, rows), BF16)),
        compiler_params=vmem(PAGE_MIB),
        cost_estimate=cost(2 * pages * slots * dim * (hidden_size + tiles * rows), 16 * MIB),
        name="page_project",
    )(lengths, document_states, projection, index)

    near, page_unit = lax.optimization_barrier((near, page_unit))
    far = swap_cores(near)
    near_best = pl.pallas_call(
        near_kernel,
        out_shape=shape((pages, chips, rows), F32),
        compiler_params=vmem(16),
        cost_estimate=cost(pages * slots * dim * tiles * rows, 2 * MIB),
        name="near_scores",
    )(near, page_unit)
    expo, keep, total, pair, target = pl.pallas_call(
        lambda *refs: far_kernel(multiplier, *refs),
        in_specs=[smem] + [pl.BlockSpec(memory_space=pltpu.VMEM)] * 4,
        out_shape=(
            shape((pages, tiles, rows), F32),
            shape((chips, dim, rows), F32),
            shape((tiles, 128), F32),
            shape((chips, dim + 16, rows), BF16),
            shape((dim, rows), F32),
        ),
        scratch_shapes=[pltpu.VMEM((pages, tiles, rows), F32)],
        compiler_params=vmem(24),
        cost_estimate=cost(pages * slots * dim * tiles * rows, 8 * MIB),
        name="far_scores",
    )(place, far, page_unit, near_best, chosen)
    send, own = pl.pallas_call(
        add_kernel,
        in_specs=[smem] + [pl.BlockSpec(memory_space=pltpu.VMEM)] * 3,
        out_shape=(shape((chips, dim + 16, rows), BF16), shape((dim, rows), F32)),
        compiler_params=vmem(8),
        name="add_pair",
    )(place, keep, total, swap_cores(pair))
    received = lax.all_to_all(send, "chip", 0, 0, tiled=True)

    weight_part, query_grad = pl.pallas_call(
        lambda *refs: gradient_kernel(multiplier, *refs),
        grid=(pages,),
        in_specs=[
            smem,
            pl.BlockSpec((1, tiles, rows), lambda i: (i, 0, 0)),
            pl.BlockSpec((1, tiles, rows), lambda i: (i, 0, 0)),
            whole((chips, dim + 16, rows)),
            whole((dim, rows)),
            whole((dim, rows)),
            whole((chips, dim, rows)),
            whole((chips, dim, rows)),
            pl.BlockSpec((1, dim, slots), lambda i: (i, 0, 0)),
            pl.BlockSpec(memory_space=pl.ANY),
            whole((dim, rows)),
            pl.BlockSpec(memory_space=pl.ANY),
        ],
        out_specs=[whole((hidden_size, dim)), whole((rows, dim))],
        out_shape=(shape((hidden_size, dim), BF16), shape((rows, dim), F32)),
        scratch_shapes=[
            pltpu.VMEM((tiles, rows), F32),
            pltpu.VMEM((tiles, rows), F32),
            pltpu.VMEM((slots // 256 * dim, 256), F32),
            pltpu.VMEM((dim, hidden_size), F32),
            pltpu.VMEM((pages, slots, hidden_size), BF16),
            pltpu.VMEM((rows, hidden_size), BF16),
            pltpu.SemaphoreType.DMA((pages + 1,)),
        ],
        compiler_params=vmem(GRADIENT_MIB),
        cost_estimate=cost(2 * pages * slots * dim * (hidden_size + tiles * rows), 16 * MIB),
        name="gradients",
    )(place, index, expo, received, own, target, near, far, page_raw, document_states, query_raw, query_rows)

    everyone = ("dp", "chip", "core")
    devices = lax.axis_size(everyone)
    chunk = hidden_size // devices
    terms = lax.all_to_all(weight_part.reshape(devices, chunk, dim), everyone, 0, 0, tiled=True)
    mine = jnp.sum(terms.astype(F32), axis=0).astype(BF16)
    shared = lax.all_to_all(jnp.broadcast_to(mine[None], (devices, chunk, dim)), everyone, 0, 0, tiled=True)
    weight_grad = shared.reshape(hidden_size, dim).astype(F32)
    return (weight_grad, query_grad.reshape(query_count, tokens, dim))


def solution(mesh):
    groups, gallery = mesh.devices.shape
    levels = Mesh(mesh.devices.reshape(groups, gallery // 2, 2), ("dp", "chip", "core"))
    every = ("dp", "chip", "core")
    return jax.shard_map(
        per_device,
        mesh=levels,
        in_specs=(P(every, None, None), P(every, None, None), P(), P(every), P("dp", None, ("chip", "core"))),
        out_specs=(P(), P(every, None, None)),
        check_vma=False,
    )
```

```python
import jax
import jax.numpy as jnp
from jax import lax
from jax.experimental import pallas as pl
from jax.experimental.pallas import tpu as pltpu
from jax.sharding import Mesh, PartitionSpec as P

F32 = jnp.float32
BF16 = jnp.bfloat16
EPSILON = 1e-06
TEMPERATURE = 0.02
MIB = 1024 * 1024
QUERY_MIB, PAGE_MIB, NEAR_MIB, FAR_MIB, GRADIENT_MIB = 60, 56, 40, 24, 14

NT = (((1,), (1,)), ((), ()))


def inverse_norm(raw):
    value = jnp.sum(raw * raw, axis=0, keepdims=True) + EPSILON
    guess = lax.rsqrt(value)
    return guess * (1.5 - 0.5 * value * guess * guess)


def unit_backward(grad_unit, raw):
    inverse = inverse_norm(raw)
    unit = raw * inverse
    return (grad_unit - unit * jnp.sum(unit * grad_unit, axis=0, keepdims=True)) * inverse


def iota(shape, axis):
    return lax.broadcasted_iota(jnp.int32, shape, axis)


def one_hot(low):
    index = low.astype(F32).astype(BF16)
    positions = iota((256, low.shape[1]), 0).astype(F32).astype(BF16)
    return jnp.where(positions == index, jnp.ones((), BF16), jnp.zeros((), BF16))


def query_kernel(hidden_any, weight_any, raw_ref, send_ref, hidden, weight, arrived):
    copies = [
        pltpu.make_async_copy(weight_any, weight, arrived.at[0]),
        pltpu.make_async_copy(hidden_any, hidden, arrived.at[1]),
    ]
    for copy in copies:
        copy.start()
    for copy in copies:
        copy.wait()
    raw = jnp.dot(hidden[...], weight[...], preferred_element_type=F32).T
    raw_ref[...] = raw
    unit = (raw * inverse_norm(raw)).astype(BF16)
    for block in range(send_ref.shape[0]):
        send_ref[block] = unit


def page_kernel(length_any, hidden_any, weight_any, best_any, raw_any, unit_any, chosen_any, index_ref,
                hidden, weight, best, length, turned, raw_ref, unit_ref, chosen_ref, arrived, left):
    pages, slots, _ = hidden.shape
    dim, tiles = weight.shape[1], index_ref.shape[1]
    parts = slots // 256
    small = [
        pltpu.make_async_copy(best_any, best, arrived.at[pages]),
        pltpu.make_async_copy(weight_any, weight, arrived.at[pages + 1]),
        pltpu.make_async_copy(length_any, length, arrived.at[pages + 2]),
    ]

    def page_copy(page):
        return pltpu.make_async_copy(hidden_any.at[page], hidden.at[page], arrived.at[page])

    def raw_copy(page):
        return pltpu.make_async_copy(raw_ref.at[page], raw_any.at[page], left.at[0, page])

    def unit_copy(page):
        return pltpu.make_async_copy(unit_ref.at[page], unit_any.at[page], left.at[1, page])

    def chosen_copy(page, part):
        some = pl.ds(part * (tiles // 2), tiles // 2)
        return pltpu.make_async_copy(chosen_ref.at[page, some], chosen_any.at[page, some], left.at[2 + part, page])

    page_copy(0).start()
    for copy in small:
        copy.start()
    page_copy(1).start()
    small[0].wait()
    for page in range(pages):
        tokens = best[:, page, :].astype(F32)
        turned[...] = jnp.concatenate([tokens, jnp.zeros((96, 128), F32)], axis=0).T
        for core in range(2):
            halves = []
            for half in range(2):
                row = jnp.zeros((8, 128), F32)
                for query in range(4):
                    piece = turned[pl.ds(core * 8 + half * 4 + query, 8, stride=16), :]
                    row = row + (pltpu.roll(piece, 32 * query, 1) if query else piece)
                halves.append(row)
            index_ref[page, core * 8:core * 8 + 8, :] = jnp.concatenate(halves, axis=1).astype(jnp.int32)
    small[1].wait()
    small[2].wait()

    def one_page(page, carry):
        page_copy(page).wait()

        @pl.when(page + 2 < pages)
        def _():
            page_copy(page + 2).start()

        raw = jnp.dot(hidden[page], weight[...], preferred_element_type=F32).T
        raw_ref[page] = raw
        raw_copy(page).start()
        unit = raw * inverse_norm(raw)
        unit_ref[page] = jnp.where(iota(unit.shape, 1) < length[page], unit, unit[:, 0:1]).T.astype(BF16)
        unit_copy(page).start()
        unit = unit.astype(BF16)
        table = jnp.concatenate([unit[:, part * 256:(part + 1) * 256] for part in range(parts)], axis=0)

        def one_tile(tile, inner):
            index = index_ref[page, pl.ds(tile, 1), :]
            found = jnp.dot(table, one_hot(index & 255), preferred_element_type=F32)
            which = index >> 8
            chosen = found[0:dim]
            for part in range(1, parts):
                chosen = jnp.where(which == part, found[part * dim:(part + 1) * dim], chosen)
            chosen_ref[page, tile] = chosen.astype(BF16)

        def half_of_tiles(part, inner):
            for tile in range(tiles // 2):
                one_tile(part * (tiles // 2) + tile, inner)
            chosen_copy(page, part).start()
            return inner

        return lax.fori_loop(0, 2, half_of_tiles, carry)

    lax.fori_loop(0, pages, one_page, 0)
    for page in range(pages):
        raw_copy(page).wait()
        unit_copy(page).wait()
        for part in range(2):
            chosen_copy(page, part).wait()


def best_scores(queries, unit_ref, out, row):
    for page in range(unit_ref.shape[0]):
        scores = jnp.dot(unit_ref[page], queries, preferred_element_type=F32)
        top = jnp.max(scores.reshape(-1, 8, scores.shape[1]), axis=0)
        out[page, pl.ds(row, 1), :] = jnp.max(top, axis=0, keepdims=True)


def near_kernel(query_ref, unit_ref, hidden_any, best_ref, hidden_ref, arrived):
    hidden_copy = pltpu.make_async_copy(hidden_any, hidden_ref, arrived)
    hidden_copy.start()

    def one_tile(tile, carry):
        best_scores(query_ref[tile], unit_ref, best_ref, tile)
        return carry

    lax.fori_loop(0, query_ref.shape[0], one_tile, 0, unroll=2)
    hidden_copy.wait()


def mixed(expo_ref, chosen_ref, tile):
    result = expo_ref[0, pl.ds(tile, 1), :] * chosen_ref[0, tile].astype(F32)
    for page in range(1, expo_ref.shape[0]):
        result = result + expo_ref[page, pl.ds(tile, 1), :] * chosen_ref[page, tile].astype(F32)
    return result


def far_kernel(multiplier, place_ref, query_ref, unit_ref, near_ref, chosen_ref, expo_ref, total_ref, pair_ref, best):
    core = place_ref[0]
    pages, chips = near_ref.shape[:2]
    dim, lanes = query_ref.shape[1:]
    near = pl.multiple_of(core * chips, chips)
    far = pl.multiple_of((1 - core) * chips, chips)
    for page in range(pages):
        best[page, pl.ds(near, chips), :] = near_ref[page]

    def one_tile(tile, carry):
        best_scores(query_ref[tile], unit_ref, best, far + tile)
        return carry

    lax.fori_loop(0, chips, one_tile, 0, unroll=2)

    segment = jnp.where(iota((lanes, lanes), 0) // 32 == iota((lanes, lanes), 1) // 32, 1.0, 0.0).astype(BF16)
    value = best[...].reshape(pages * 2 * chips, lanes)
    score = jnp.zeros_like(value)
    for _ in range(3):
        part = value.astype(BF16)
        score = score + jnp.dot(part, segment, preferred_element_type=F32)
        value = value - part.astype(F32)
    expo = jnp.exp(score * multiplier).reshape(pages, 2 * chips, lanes)
    expo_ref[...] = expo
    total = jnp.sum(expo, axis=0)
    total = jnp.where(iota((2 * chips, 128), 1) % 32 < 16, total[:, :128], total[:, 128:])
    total_ref[...] = total
    high = total.astype(BF16)
    low = (total - high.astype(F32)).astype(BF16)

    def one_mix(tile, carry):
        pair_ref[tile, 0:dim, :] = mixed(expo_ref, chosen_ref, far + tile).astype(BF16)
        pair_ref[tile, dim:dim + 16, 0:128] = high
        pair_ref[tile, dim:dim + 16, 128:256] = low
        return carry

    lax.fori_loop(0, chips, one_mix, 0, unroll=2)


def keep_kernel(place_ref, expo_ref, chosen_ref, keep_ref, target_ref):
    core, chip = place_ref[0], place_ref[1]
    chips, dim, lanes = keep_ref.shape
    near = core * chips

    def one_mix(tile, carry):
        keep_ref[tile] = mixed(expo_ref, chosen_ref, near + tile)
        return carry

    lax.fori_loop(0, chips, one_mix, 0, unroll=2)
    picked = jnp.zeros((dim, lanes), F32)
    for page in range(expo_ref.shape[0]):
        picked = jnp.where(iota((dim, lanes), 1) // 64 == page, chosen_ref[page, near + chip].astype(F32), picked)
    target_ref[...] = picked


def add_kernel(place_ref, keep_ref, total_ref, pair_ref, send_ref, own_ref):
    chips, dim, _ = keep_ref.shape
    total = total_ref[...] + (pair_ref[0, dim:dim + 16, 0:128].astype(F32) + pair_ref[0, dim:dim + 16, 128:256].astype(F32))
    high = total.astype(BF16)
    low = (total - high.astype(F32)).astype(BF16)
    for tile in range(chips):
        send_ref[tile, 0:dim, :] = (keep_ref[tile] + pair_ref[tile, 0:dim, :].astype(F32)).astype(BF16)
        send_ref[tile, dim:dim + 16, 0:128] = high
        send_ref[tile, dim:dim + 16, 128:256] = low
    chip = place_ref[1]
    own_ref[...] = keep_ref[chip] + pair_ref[chip, 0:dim, :].astype(F32)


def gradient_kernel(multiplier, place_ref, index_ref, expo_ref, received_ref, own_ref, target_ref, near_ref, far_ref, page_raw,
                    hidden, query_raw_ref, query_hidden, keep_ref, give_ref, query_grad_ref, inverse_total, score_grad, summed_grad,
                    accumulated, turned):
    core, chip = place_ref[0], place_ref[1]
    chips, dim, lanes = near_ref.shape
    tiles = 2 * chips
    mine = core * chips + chip
    pages, slots, _ = hidden.shape
    parts = slots // 256
    total = jnp.zeros((tiles, 128), F32)
    for source in range(chips):
        total = total + received_ref[source, dim:dim + 16, 0:128].astype(F32) + received_ref[source, dim:dim + 16, 128:256].astype(F32)
    inverse = 1.0 / total
    first = iota((tiles, 128), 1) % 32 < 16
    inverse_total[:, 0:128] = jnp.where(first, inverse, pltpu.roll(inverse, 16, 1))
    inverse_total[:, 128:256] = jnp.where(first, pltpu.roll(inverse, 112, 1), inverse)
    accumulated[...] = jnp.zeros_like(accumulated)

    def one_page(page, carry):
        is_target = (iota((tiles, lanes), 0) == mine) & (iota((tiles, lanes), 1) // 64 == page)
        score_grad[...] = (expo_ref[page] * inverse_total[...] - jnp.where(is_target, 1.0, 0.0)) * multiplier
        for side, queries_ref in ((core, near_ref), (1 - core, far_ref)):
            for chip_of in range(chips):
                tile = side * chips + chip_of
                index = index_ref[page, pl.ds(tile, 1), :]
                weighted = queries_ref[chip_of].astype(F32) * score_grad[pl.ds(tile, 1), :]
                which = index >> 8
                left = jnp.concatenate([jnp.where(which == part, weighted, 0.0).astype(BF16) for part in range(parts)], axis=0)
                term = lax.dot_general(left, one_hot(index & 255), NT, preferred_element_type=F32)
                if queries_ref is near_ref and chip_of == 0:
                    summed_grad[...] = term
                else:
                    summed_grad[...] += term
        grad = jnp.concatenate([summed_grad[part * dim:(part + 1) * dim] for part in range(parts)], axis=1)
        direction = unit_backward(grad, page_raw[page]).astype(BF16)
        accumulated[...] += jnp.dot(direction, hidden[page], preferred_element_type=F32)
        return carry

    lax.fori_loop(0, pages, one_page, 0)
    summed = own_ref[...]
    for source in range(chips):
        summed = summed + jnp.where(chip == source, 0.0, received_ref[source, 0:dim, :].astype(F32))
    query_grad = (summed * inverse_total[pl.ds(mine, 1), :] - target_ref[...]) * multiplier
    query_grad_ref[...] = query_grad.T
    direction = unit_backward(query_grad, query_raw_ref[...]).astype(BF16)
    turned[...] = (accumulated[...] + jnp.dot(direction, query_hidden[...], preferred_element_type=F32)).T
    half = keep_ref.shape[0]
    keep_ref[...] = turned[pl.ds(pl.multiple_of(core * half, half), half), :]
    give_ref[...] = turned[pl.ds(pl.multiple_of((1 - core) * half, half), half), :].astype(BF16)


def shape(dims, kind):
    return jax.ShapeDtypeStruct(dims, kind)


def vmem(mib):
    return pltpu.CompilerParams(vmem_limit_bytes=mib * MIB)


def cost(flops, read):
    return pl.CostEstimate(flops=flops, bytes_accessed=read, transcendentals=0)


def swap_cores(value):
    return lax.ppermute(value, "core", [(0, 1), (1, 0)])


def summed(terms):
    return lax.optimization_barrier(jnp.sum(terms.astype(F32), axis=0)).astype(BF16)


def to_all(value, axis):
    return lax.all_to_all(jnp.broadcast_to(value[None], (lax.axis_size(axis),) + value.shape), axis, 0, 0, tiled=True)


def per_device(query_hidden, document_states, projection, lengths, best_token):
    query_count, tokens, hidden_size = query_hidden.shape
    pages, slots, _ = document_states.shape
    dim = projection.shape[1]
    chips, cores = lax.axis_size("chip"), lax.axis_size("core")
    tiles = chips * cores
    rows = query_count * tokens
    multiplier = 1.0 / (tokens * TEMPERATURE)
    smem = pl.BlockSpec(memory_space=pltpu.SMEM)
    inside = pl.BlockSpec(memory_space=pltpu.VMEM)
    anywhere = pl.BlockSpec(memory_space=pl.ANY)
    place = jnp.stack([lax.axis_index("core"), lax.axis_index("chip")]).astype(jnp.int32)
    query_rows = query_hidden.reshape(rows, hidden_size)

    query_raw, query_send = pl.pallas_call(
        query_kernel,
        in_specs=[anywhere] * 2,
        out_shape=(shape((dim, rows), F32), shape((chips, dim, rows), BF16)),
        scratch_shapes=[pltpu.VMEM((rows, hidden_size), BF16), pltpu.VMEM((hidden_size, dim), BF16), pltpu.SemaphoreType.DMA((2,))],
        compiler_params=vmem(QUERY_MIB),
        cost_estimate=cost(2 * rows * hidden_size * dim, 2 * MIB),
        name="query_project",
    )(query_rows, projection)
    near = lax.all_to_all(query_send, "chip", 0, 0, tiled=True)

    page_raw, page_unit, chosen, index = pl.pallas_call(
        page_kernel,
        in_specs=[anywhere] * 4,
        out_specs=[anywhere] * 3 + [inside],
        out_shape=(
            shape((pages, dim, slots), F32),
            shape((pages, slots, dim), BF16),
            shape((pages, tiles, dim, rows), BF16),
            shape((pages, tiles, rows), jnp.int32),
        ),
        scratch_shapes=[
            pltpu.VMEM((pages, slots, hidden_size), BF16),
            pltpu.VMEM((hidden_size, dim), BF16),
            pltpu.VMEM((tokens, pages, chips * cores * query_count), jnp.int32),
            pltpu.SMEM((pages,), jnp.int32),
            pltpu.VMEM((128, 128), F32),
            pltpu.VMEM((pages, dim, slots), F32),
            pltpu.VMEM((pages, slots, dim), BF16),
            pltpu.VMEM((pages, tiles, dim, rows), BF16),
            pltpu.SemaphoreType.DMA((pages + 3,)),
            pltpu.SemaphoreType.DMA((4, pages)),
        ],
        compiler_params=vmem(PAGE_MIB),
        cost_estimate=cost(2 * pages * slots * dim * (hidden_size + tiles * rows), 16 * MIB),
        name="page_project",
    )(lengths, document_states, projection, jnp.transpose(best_token, (1, 2, 0)))

    near, index = lax.optimization_barrier((near, index))
    far = swap_cores(near)
    near_best, page_hidden = pl.pallas_call(
        near_kernel,
        in_specs=[inside] * 2 + [anywhere],
        out_shape=(shape((pages, chips, rows), F32), shape((pages, slots, hidden_size), BF16)),
        scratch_shapes=[pltpu.SemaphoreType.DMA],
        compiler_params=vmem(NEAR_MIB),
        cost_estimate=cost(pages * slots * dim * tiles * rows, 2 * MIB),
        name="near_scores",
    )(near, page_unit, document_states)
    expo, total, pair = pl.pallas_call(
        lambda *refs: far_kernel(multiplier, *refs),
        in_specs=[smem] + [inside] * 4,
        out_shape=(shape((pages, tiles, rows), F32), shape((tiles, 128), F32), shape((chips, dim + 16, rows), BF16)),
        scratch_shapes=[pltpu.VMEM((pages, tiles, rows), F32)],
        compiler_params=vmem(FAR_MIB),
        cost_estimate=cost(pages * slots * dim * tiles * rows, 8 * MIB),
        name="far_scores",
    )(place, far, page_unit, near_best, chosen)
    keep, target = pl.pallas_call(
        keep_kernel,
        in_specs=[smem] + [inside] * 2,
        out_shape=(shape((chips, dim, rows), F32), shape((dim, rows), F32)),
        compiler_params=vmem(24),
        cost_estimate=cost(2 * pages * dim * tiles * rows, 4 * MIB),
        name="keep_terms",
    )(place, expo, chosen)
    send, own = pl.pallas_call(
        add_kernel,
        in_specs=[smem] + [inside] * 3,
        out_shape=(shape((chips, dim + 16, rows), BF16), shape((dim, rows), F32)),
        compiler_params=vmem(8),
        name="add_pair",
    )(place, keep, total, swap_cores(pair))
    received = lax.all_to_all(send, "chip", 0, 0, tiled=True)

    half = hidden_size // cores
    weight_keep, weight_give, query_grad = pl.pallas_call(
        lambda *refs: gradient_kernel(multiplier, *refs),
        in_specs=[smem] + [inside] * 11,
        out_shape=(shape((half, dim), F32), shape((half, dim), BF16), shape((rows, dim), F32)),
        scratch_shapes=[
            pltpu.VMEM((tiles, rows), F32),
            pltpu.VMEM((tiles, rows), F32),
            pltpu.VMEM((slots // 256 * dim, 256), F32),
            pltpu.VMEM((dim, hidden_size), F32),
            pltpu.VMEM((hidden_size, dim), F32),
        ],
        compiler_params=vmem(GRADIENT_MIB),
        cost_estimate=cost(2 * pages * slots * dim * (hidden_size + tiles * rows), 16 * MIB),
        name="gradients",
    )(place, index, expo, received, own, target, near, far, page_raw, page_hidden, query_raw, query_rows)

    halves = (weight_keep + swap_cores(weight_give).astype(F32)).astype(BF16)
    chunk = summed(lax.all_to_all(halves.reshape(chips, half // chips, dim), "chip", 0, 0, tiled=True))
    chunk = summed(to_all(chunk, "dp"))
    mine = to_all(chunk, "chip").reshape(half, dim)
    other = swap_cores(mine)
    first = lax.axis_index("core") == 0
    weight_grad = jnp.concatenate([jnp.where(first, mine, other), jnp.where(first, other, mine)], axis=0).astype(F32)
    return (weight_grad, query_grad.reshape(query_count, tokens, dim))


def solution(mesh):
    groups, gallery = mesh.devices.shape
    levels = Mesh(mesh.devices.reshape(groups, gallery // 2, 2), ("dp", "chip", "core"))
    every = ("dp", "chip", "core")
    return jax.shard_map(
        per_device,
        mesh=levels,
        in_specs=(P(every, None, None), P(every, None, None), P(), P(every), P("dp", None, ("chip", "core"))),
        out_specs=(P(), P(every, None, None)),
        check_vma=False,
    )
```

```python
import jax
import jax.numpy as jnp
from jax import lax
from jax.experimental import pallas as pl
from jax.experimental.pallas import tpu as pltpu
from jax.sharding import Mesh, PartitionSpec as P

F32 = jnp.float32
BF16 = jnp.bfloat16
EPSILON = 1e-06
TEMPERATURE = 0.02
MIB = 1024 * 1024
QUERY_MIB, PAGE_MIB, NEAR_MIB, FAR_MIB, GRADIENT_MIB = 60, 56, 40, 24, 14

NT = (((1,), (1,)), ((), ()))


def inverse_norm(raw):
    value = jnp.sum(raw * raw, axis=0, keepdims=True) + EPSILON
    guess = lax.rsqrt(value)
    return guess * (1.5 - 0.5 * value * guess * guess)


def unit_backward(grad_unit, raw):
    inverse = inverse_norm(raw)
    unit = raw * inverse
    return (grad_unit - unit * jnp.sum(unit * grad_unit, axis=0, keepdims=True)) * inverse


def iota(shape, axis):
    return lax.broadcasted_iota(jnp.int32, shape, axis)


def one_hot(low):
    index = low.astype(F32).astype(BF16)
    positions = iota((256, low.shape[1]), 0).astype(F32).astype(BF16)
    return jnp.where(positions == index, jnp.ones((), BF16), jnp.zeros((), BF16))


def query_kernel(hidden_any, weight_any, raw_ref, send_ref, hidden, weight, arrived):
    copies = [
        pltpu.make_async_copy(weight_any, weight, arrived.at[0]),
        pltpu.make_async_copy(hidden_any, hidden, arrived.at[1]),
    ]
    for copy in copies:
        copy.start()
    for copy in copies:
        copy.wait()
    raw = jnp.dot(hidden[...], weight[...], preferred_element_type=F32).T
    raw_ref[...] = raw
    unit = (raw * inverse_norm(raw)).astype(BF16)
    for block in range(send_ref.shape[0]):
        send_ref[block] = unit


def page_kernel(length_any, hidden_any, weight_any, best_any, raw_any, unit_any, chosen_any, index_ref,
                hidden, weight, best, length, turned, raw_ref, unit_ref, chosen_ref, arrived, left):
    pages, slots, _ = hidden.shape
    dim, tiles = weight.shape[1], index_ref.shape[1]
    parts = slots // 256
    small = [
        pltpu.make_async_copy(best_any, best, arrived.at[pages]),
        pltpu.make_async_copy(weight_any, weight, arrived.at[pages + 1]),
        pltpu.make_async_copy(length_any, length, arrived.at[pages + 2]),
    ]

    def page_copy(page):
        return pltpu.make_async_copy(hidden_any.at[page], hidden.at[page], arrived.at[page])

    def raw_copy(page):
        return pltpu.make_async_copy(raw_ref.at[page], raw_any.at[page], left.at[0, page])

    def unit_copy(page):
        return pltpu.make_async_copy(unit_ref.at[page], unit_any.at[page], left.at[1, page])

    def chosen_copy(page, part):
        some = pl.ds(part * (tiles // 2), tiles // 2)
        return pltpu.make_async_copy(chosen_ref.at[page, some], chosen_any.at[page, some], left.at[2 + part, page])

    page_copy(0).start()
    for copy in small:
        copy.start()
    page_copy(1).start()
    small[0].wait()
    for page in range(pages):
        tokens = best[:, page, :].astype(F32)
        turned[...] = jnp.concatenate([tokens, jnp.zeros((96, 128), F32)], axis=0).T
        for core in range(2):
            halves = []
            for half in range(2):
                row = jnp.zeros((8, 128), F32)
                for query in range(4):
                    piece = turned[pl.ds(core * 8 + half * 4 + query, 8, stride=16), :]
                    row = row + (pltpu.roll(piece, 32 * query, 1) if query else piece)
                halves.append(row)
            index_ref[page, core * 8:core * 8 + 8, :] = jnp.concatenate(halves, axis=1).astype(jnp.int32)
    small[1].wait()
    small[2].wait()

    def project(page):
        page_copy(page).wait()
        if page + 2 < pages:
            page_copy(page + 2).start()
        raw_ref[page] = jnp.dot(hidden[page], weight[...], preferred_element_type=F32).T
        raw_copy(page).start()

    project(0)
    for page in range(pages):
        if page + 1 < pages:
            project(page + 1)
        raw = raw_ref[page]
        unit = raw * inverse_norm(raw)
        unit_ref[page] = jnp.where(iota(unit.shape, 1) < length[page], unit, unit[:, 0:1]).T.astype(BF16)
        unit_copy(page).start()
        unit = unit.astype(BF16)
        table = jnp.concatenate([unit[:, part * 256:(part + 1) * 256] for part in range(parts)], axis=0)

        for tile in range(tiles):
            index = index_ref[page, tile:tile + 1, :]
            found = jnp.dot(table, one_hot(index & 255), preferred_element_type=F32)
            which = index >> 8
            chosen = found[0:dim]
            for part in range(1, parts):
                chosen = jnp.where(which == part, found[part * dim:(part + 1) * dim], chosen)
            chosen_ref[page, tile] = chosen.astype(BF16)
            if (tile + 1) % (tiles // 2) == 0:
                chosen_copy(page, tile // (tiles // 2)).start()
    for page in range(pages):
        raw_copy(page).wait()
        unit_copy(page).wait()
        for part in range(2):
            chosen_copy(page, part).wait()


def best_scores(queries, unit_ref, out, row):
    for page in range(unit_ref.shape[0]):
        scores = jnp.dot(unit_ref[page], queries, preferred_element_type=F32)
        top = jnp.max(scores.reshape(-1, 8, scores.shape[1]), axis=0)
        out[page, pl.ds(row, 1), :] = jnp.max(top, axis=0, keepdims=True)


def near_kernel(query_ref, unit_ref, hidden_any, best_ref, hidden_ref, arrived):
    hidden_copy = pltpu.make_async_copy(hidden_any, hidden_ref, arrived)
    hidden_copy.start()

    for tile in range(query_ref.shape[0]):
        best_scores(query_ref[tile], unit_ref, best_ref, tile)
    hidden_copy.wait()


def mixed(expo_ref, chosen_ref, tile):
    result = expo_ref[0, pl.ds(tile, 1), :] * chosen_ref[0, tile].astype(F32)
    for page in range(1, expo_ref.shape[0]):
        result = result + expo_ref[page, pl.ds(tile, 1), :] * chosen_ref[page, tile].astype(F32)
    return result


def far_kernel(multiplier, place_ref, query_ref, unit_ref, near_ref, chosen_ref, expo_ref, total_ref, pair_ref, best):
    core = place_ref[0]
    pages, chips = near_ref.shape[:2]
    dim, lanes = query_ref.shape[1:]
    near = pl.multiple_of(core * chips, chips)
    far = pl.multiple_of((1 - core) * chips, chips)
    for page in range(pages):
        best[page, pl.ds(near, chips), :] = near_ref[page]

    for tile in range(chips):
        best_scores(query_ref[tile], unit_ref, best, far + tile)

    segment = jnp.where(iota((lanes, lanes), 0) // 32 == iota((lanes, lanes), 1) // 32, 1.0, 0.0).astype(BF16)
    value = best[...].reshape(pages * 2 * chips, lanes)
    score = jnp.zeros_like(value)
    for _ in range(3):
        part = value.astype(BF16)
        score = score + jnp.dot(part, segment, preferred_element_type=F32)
        value = value - part.astype(F32)
    expo = jnp.exp(score * multiplier).reshape(pages, 2 * chips, lanes)
    expo_ref[...] = expo
    total = jnp.sum(expo, axis=0)
    total = jnp.where(iota((2 * chips, 128), 1) % 32 < 16, total[:, :128], total[:, 128:])
    total_ref[...] = total
    high = total.astype(BF16)
    low = (total - high.astype(F32)).astype(BF16)

    def one_mix(tile, carry):
        pair_ref[tile, 0:dim, :] = mixed(expo_ref, chosen_ref, far + tile).astype(BF16)
        pair_ref[tile, dim:dim + 16, 0:128] = high
        pair_ref[tile, dim:dim + 16, 128:256] = low
        return carry

    lax.fori_loop(0, chips, one_mix, 0, unroll=2)


def keep_kernel(place_ref, expo_ref, chosen_ref, keep_ref, target_ref):
    core, chip = place_ref[0], place_ref[1]
    chips, dim, lanes = keep_ref.shape
    near = core * chips

    def one_mix(tile, carry):
        keep_ref[tile] = mixed(expo_ref, chosen_ref, near + tile)
        return carry

    lax.fori_loop(0, chips, one_mix, 0, unroll=2)
    picked = jnp.zeros((dim, lanes), F32)
    for page in range(expo_ref.shape[0]):
        picked = jnp.where(iota((dim, lanes), 1) // 64 == page, chosen_ref[page, near + chip].astype(F32), picked)
    target_ref[...] = picked


def add_kernel(place_ref, keep_ref, total_ref, pair_ref, send_ref, own_ref):
    chips, dim, _ = keep_ref.shape
    total = total_ref[...] + (pair_ref[0, dim:dim + 16, 0:128].astype(F32) + pair_ref[0, dim:dim + 16, 128:256].astype(F32))
    high = total.astype(BF16)
    low = (total - high.astype(F32)).astype(BF16)
    for tile in range(chips):
        send_ref[tile, 0:dim, :] = (keep_ref[tile] + pair_ref[tile, 0:dim, :].astype(F32)).astype(BF16)
        send_ref[tile, dim:dim + 16, 0:128] = high
        send_ref[tile, dim:dim + 16, 128:256] = low
    chip = place_ref[1]
    own_ref[...] = keep_ref[chip] + pair_ref[chip, 0:dim, :].astype(F32)


def gradient_kernel(multiplier, place_ref, index_ref, expo_ref, received_ref, own_ref, target_ref, near_ref, far_ref, page_raw,
                    hidden, query_raw_ref, query_hidden, keep_ref, give_ref, query_grad_ref, inverse_total, score_grad, summed_grad,
                    accumulated, turned):
    core, chip = place_ref[0], place_ref[1]
    chips, dim, lanes = near_ref.shape
    tiles = 2 * chips
    mine = core * chips + chip
    pages, slots, _ = hidden.shape
    parts = slots // 256
    total = jnp.zeros((tiles, 128), F32)
    for source in range(chips):
        total = total + received_ref[source, dim:dim + 16, 0:128].astype(F32) + received_ref[source, dim:dim + 16, 128:256].astype(F32)
    inverse = 1.0 / total
    first = iota((tiles, 128), 1) % 32 < 16
    inverse_total[:, 0:128] = jnp.where(first, inverse, pltpu.roll(inverse, 16, 1))
    inverse_total[:, 128:256] = jnp.where(first, pltpu.roll(inverse, 112, 1), inverse)
    accumulated[...] = jnp.zeros_like(accumulated)

    def scattered(page, tile, weighted):
        index = index_ref[page, pl.ds(tile, 1), :]
        which = index >> 8
        left = jnp.concatenate([jnp.where(which == part, weighted, 0.0).astype(BF16) for part in range(parts)], axis=0)
        return lax.dot_general(left, one_hot(index & 255), NT, preferred_element_type=F32)

    for page in range(pages):
        is_target = (iota((tiles, lanes), 0) == mine) & (iota((tiles, lanes), 1) // 64 == page)
        score_grad[...] = (expo_ref[page] * inverse_total[...] - jnp.where(is_target, 1.0, 0.0)) * multiplier
        weighted = near_ref[chip].astype(F32) * score_grad[pl.ds(mine, 1), :]
        summed_grad[...] = scattered(page, mine, weighted - weighted.astype(BF16).astype(F32))
        for side, queries_ref in ((core, near_ref), (1 - core, far_ref)):
            for chip_of in range(chips):
                tile = side * chips + chip_of
                summed_grad[...] += scattered(page, tile, queries_ref[chip_of].astype(F32) * score_grad[pl.ds(tile, 1), :])
        grad = jnp.concatenate([summed_grad[part * dim:(part + 1) * dim] for part in range(parts)], axis=1)
        direction = unit_backward(grad, page_raw[page]).astype(BF16)
        accumulated[...] += jnp.dot(direction, hidden[page], preferred_element_type=F32)
    summed = own_ref[...]
    for source in range(chips):
        summed = summed + jnp.where(chip == source, 0.0, received_ref[source, 0:dim, :].astype(F32))
    query_grad = (summed * inverse_total[pl.ds(mine, 1), :] - target_ref[...]) * multiplier
    query_grad_ref[...] = query_grad.T
    direction = unit_backward(query_grad, query_raw_ref[...]).astype(BF16)
    turned[...] = (accumulated[...] + jnp.dot(direction, query_hidden[...], preferred_element_type=F32)).T
    half = keep_ref.shape[0]
    keep_ref[...] = turned[pl.ds(pl.multiple_of(core * half, half), half), :]
    give_ref[...] = turned[pl.ds(pl.multiple_of((1 - core) * half, half), half), :]


def shape(dims, kind):
    return jax.ShapeDtypeStruct(dims, kind)


def vmem(mib):
    return pltpu.CompilerParams(vmem_limit_bytes=mib * MIB)


def cost(flops, read):
    return pl.CostEstimate(flops=flops, bytes_accessed=read, transcendentals=0)


def swap_cores(value):
    return lax.ppermute(value, "core", [(0, 1), (1, 0)])


def summed(terms):
    return lax.optimization_barrier(jnp.sum(terms.astype(F32), axis=0)).astype(BF16)


def to_all(value, axis):
    return lax.all_to_all(jnp.broadcast_to(value[None], (lax.axis_size(axis),) + value.shape), axis, 0, 0, tiled=True)


def per_device(query_hidden, document_states, projection, lengths, best_token):
    query_count, tokens, hidden_size = query_hidden.shape
    pages, slots, _ = document_states.shape
    dim = projection.shape[1]
    chips, cores = lax.axis_size("chip"), lax.axis_size("core")
    tiles = chips * cores
    rows = query_count * tokens
    multiplier = 1.0 / (tokens * TEMPERATURE)
    smem = pl.BlockSpec(memory_space=pltpu.SMEM)
    inside = pl.BlockSpec(memory_space=pltpu.VMEM)
    anywhere = pl.BlockSpec(memory_space=pl.ANY)
    place = jnp.stack([lax.axis_index("core"), lax.axis_index("chip")]).astype(jnp.int32)
    query_rows = query_hidden.reshape(rows, hidden_size)

    query_raw, query_send = pl.pallas_call(
        query_kernel,
        in_specs=[anywhere] * 2,
        out_shape=(shape((dim, rows), F32), shape((chips, dim, rows), BF16)),
        scratch_shapes=[pltpu.VMEM((rows, hidden_size), BF16), pltpu.VMEM((hidden_size, dim), BF16), pltpu.SemaphoreType.DMA((2,))],
        compiler_params=vmem(QUERY_MIB),
        cost_estimate=cost(2 * rows * hidden_size * dim, 2 * MIB),
        name="query_project",
    )(query_rows, projection)
    near = lax.all_to_all(query_send, "chip", 0, 0, tiled=True)

    page_raw, page_unit, chosen, index = pl.pallas_call(
        page_kernel,
        in_specs=[anywhere] * 4,
        out_specs=[anywhere] * 3 + [inside],
        out_shape=(
            shape((pages, dim, slots), F32),
            shape((pages, slots, dim), BF16),
            shape((pages, tiles, dim, rows), BF16),
            shape((pages, tiles, rows), jnp.int32),
        ),
        scratch_shapes=[
            pltpu.VMEM((pages, slots, hidden_size), BF16),
            pltpu.VMEM((hidden_size, dim), BF16),
            pltpu.VMEM((tokens, pages, chips * cores * query_count), jnp.int32),
            pltpu.SMEM((pages,), jnp.int32),
            pltpu.VMEM((128, 128), F32),
            pltpu.VMEM((pages, dim, slots), F32),
            pltpu.VMEM((pages, slots, dim), BF16),
            pltpu.VMEM((pages, tiles, dim, rows), BF16),
            pltpu.SemaphoreType.DMA((pages + 3,)),
            pltpu.SemaphoreType.DMA((4, pages)),
        ],
        compiler_params=vmem(PAGE_MIB),
        cost_estimate=cost(2 * pages * slots * dim * (hidden_size + tiles * rows), 16 * MIB),
        name="page_project",
    )(lengths, document_states, projection, jnp.transpose(best_token, (1, 2, 0)))

    near, index = lax.optimization_barrier((near, index))
    far = swap_cores(near)
    near_best, page_hidden = pl.pallas_call(
        near_kernel,
        in_specs=[inside] * 2 + [anywhere],
        out_shape=(shape((pages, chips, rows), F32), shape((pages, slots, hidden_size), BF16)),
        scratch_shapes=[pltpu.SemaphoreType.DMA],
        compiler_params=vmem(NEAR_MIB),
        cost_estimate=cost(pages * slots * dim * tiles * rows, 2 * MIB),
        name="near_scores",
    )(near, page_unit, document_states)
    expo, total, pair = pl.pallas_call(
        lambda *refs: far_kernel(multiplier, *refs),
        in_specs=[smem] + [inside] * 4,
        out_shape=(shape((pages, tiles, rows), F32), shape((tiles, 128), F32), shape((chips, dim + 16, rows), BF16)),
        scratch_shapes=[pltpu.VMEM((pages, tiles, rows), F32)],
        compiler_params=vmem(FAR_MIB),
        cost_estimate=cost(pages * slots * dim * tiles * rows, 8 * MIB),
        name="far_scores",
    )(place, far, page_unit, near_best, chosen)
    keep, target = pl.pallas_call(
        keep_kernel,
        in_specs=[smem] + [inside] * 2,
        out_shape=(shape((chips, dim, rows), F32), shape((dim, rows), F32)),
        compiler_params=vmem(24),
        cost_estimate=cost(2 * pages * dim * tiles * rows, 4 * MIB),
        name="keep_terms",
    )(place, expo, chosen)
    send, own = pl.pallas_call(
        add_kernel,
        in_specs=[smem] + [inside] * 3,
        out_shape=(shape((chips, dim + 16, rows), BF16), shape((dim, rows), F32)),
        compiler_params=vmem(8),
        name="add_pair",
    )(place, keep, total, swap_cores(pair))
    received = lax.all_to_all(send, "chip", 0, 0, tiled=True)

    half = hidden_size // cores
    weight_keep, weight_give, query_grad = pl.pallas_call(
        lambda *refs: gradient_kernel(multiplier, *refs),
        in_specs=[smem] + [inside] * 11,
        out_shape=(shape((half, dim), F32), shape((half, dim), F32), shape((rows, dim), F32)),
        scratch_shapes=[
            pltpu.VMEM((tiles, rows), F32),
            pltpu.VMEM((tiles, rows), F32),
            pltpu.VMEM((slots // 256 * dim, 256), F32),
            pltpu.VMEM((dim, hidden_size), F32),
            pltpu.VMEM((hidden_size, dim), F32),
        ],
        compiler_params=vmem(GRADIENT_MIB),
        cost_estimate=cost(2 * pages * slots * dim * (hidden_size + tiles * rows), 16 * MIB),
        name="gradients",
    )(place, index, expo, received, own, target, near, far, page_raw, page_hidden, query_raw, query_rows)

    halves = (weight_keep + swap_cores(weight_give)).astype(BF16)
    chunk = summed(lax.all_to_all(halves.reshape(chips, half // chips, dim), "chip", 0, 0, tiled=True))
    chunk = summed(to_all(chunk, "dp"))
    mine = to_all(chunk, "chip").reshape(half, dim)
    other = swap_cores(mine)
    first = lax.axis_index("core") == 0
    weight_grad = jnp.concatenate([jnp.where(first, mine, other), jnp.where(first, other, mine)], axis=0).astype(F32)
    return (weight_grad, query_grad.reshape(query_count, tokens, dim))


def solution(mesh):
    groups, gallery = mesh.devices.shape
    levels = Mesh(mesh.devices.reshape(groups, gallery // 2, 2), ("dp", "chip", "core"))
    every = ("dp", "chip", "core")
    return jax.shard_map(
        per_device,
        mesh=levels,
        in_specs=(P(every, None, None), P(every, None, None), P(), P(every), P("dp", None, ("chip", "core"))),
        out_specs=(P(), P(every, None, None)),
        check_vma=False,
    )
```

```python
import jax
import jax.numpy as jnp
from jax import lax
from jax.experimental import pallas as pl
from jax.experimental.pallas import tpu as pltpu
from jax.sharding import Mesh, PartitionSpec as P

F32 = jnp.float32
BF16 = jnp.bfloat16
EPSILON = 1e-06
TEMPERATURE = 0.02
MIB = 1024 * 1024
QUERY_MIB, PAGE_MIB, NEAR_MIB, FAR_MIB, GRADIENT_MIB = 60, 56, 40, 24, 14

NT = (((1,), (1,)), ((), ()))


def inverse_norm(raw):
    value = jnp.sum(raw * raw, axis=0, keepdims=True) + EPSILON
    guess = lax.rsqrt(value)
    return guess * (1.5 - 0.5 * value * guess * guess)


def unit_backward(grad_unit, raw):
    inverse = inverse_norm(raw)
    unit = raw * inverse
    return (grad_unit - unit * jnp.sum(unit * grad_unit, axis=0, keepdims=True)) * inverse


def iota(shape, axis):
    return lax.broadcasted_iota(jnp.int32, shape, axis)


def one_hot(low):
    index = low.astype(F32).astype(BF16)
    positions = iota((256, low.shape[1]), 0).astype(F32).astype(BF16)
    return jnp.where(positions == index, jnp.ones((), BF16), jnp.zeros((), BF16))


def query_kernel(hidden_any, weight_any, raw_ref, send_ref, hidden, weight, arrived):
    copies = [
        pltpu.make_async_copy(weight_any, weight, arrived.at[0]),
        pltpu.make_async_copy(hidden_any, hidden, arrived.at[1]),
    ]
    for copy in copies:
        copy.start()
    for copy in copies:
        copy.wait()
    raw = jnp.dot(hidden[...], weight[...], preferred_element_type=F32).T
    raw_ref[...] = raw
    unit = (raw * inverse_norm(raw)).astype(BF16)
    for block in range(send_ref.shape[0]):
        send_ref[block] = unit


def page_kernel(length_any, hidden_any, weight_any, best_any, raw_any, unit_any, chosen_any, index_any,
                hidden, weight, best, length, turned, raw_ref, unit_ref, chosen_ref, index_ref, arrived, left, index_left):
    pages, slots, _ = hidden.shape
    dim, tiles = weight.shape[1], index_ref.shape[1]
    parts = slots // 256
    small = [
        pltpu.make_async_copy(best_any, best, arrived.at[pages]),
        pltpu.make_async_copy(weight_any, weight, arrived.at[pages + 1]),
        pltpu.make_async_copy(length_any, length, arrived.at[pages + 2]),
    ]

    def page_copy(page):
        return pltpu.make_async_copy(hidden_any.at[page], hidden.at[page], arrived.at[page])

    def first_copy(part):
        some = pl.ds(part * slots // 2, slots // 2)
        return pltpu.make_async_copy(hidden_any.at[0, some], hidden.at[0, some], arrived.at[pages + 2 + part if part else 0])

    def raw_copy(page):
        return pltpu.make_async_copy(raw_ref.at[page], raw_any.at[page], left.at[0, page])

    def unit_copy(page):
        return pltpu.make_async_copy(unit_ref.at[page], unit_any.at[page], left.at[1, page])

    def chosen_copy(page, part):
        some = pl.ds(part * (tiles // 2), tiles // 2)
        return pltpu.make_async_copy(chosen_ref.at[page, some], chosen_any.at[page, some], left.at[2 + part, page])

    first_copy(0).start()
    for copy in small:
        copy.start()
    first_copy(1).start()
    page_copy(1).start()
    small[0].wait()
    for page in range(pages):
        tokens = best[:, page, :].astype(F32)
        turned[...] = jnp.concatenate([tokens, jnp.zeros((96, 128), F32)], axis=0).T
        for core in range(2):
            halves = []
            for half in range(2):
                row = jnp.zeros((8, 128), F32)
                for query in range(4):
                    piece = turned[pl.ds(core * 8 + half * 4 + query, 8, stride=16), :]
                    row = row + (pltpu.roll(piece, 32 * query, 1) if query else piece)
                halves.append(row)
            index_ref[page, core * 8:core * 8 + 8, :] = jnp.concatenate(halves, axis=1).astype(jnp.int32)
    index_copy = pltpu.make_async_copy(index_ref, index_any, index_left)
    index_copy.start()
    small[1].wait()
    small[2].wait()

    def project(page):
        if page + 2 < pages:
            page_copy(page + 2).start()
        if page:
            page_copy(page).wait()
            raw_ref[page] = jnp.dot(hidden[page], weight[...], preferred_element_type=F32).T
        else:
            for part in range(2):
                some = slice(part * slots // 2, (part + 1) * slots // 2)
                first_copy(part).wait()
                raw_ref[0, :, some] = jnp.dot(hidden[0, some], weight[...], preferred_element_type=F32).T
        raw_copy(page).start()

    project(0)
    for page in range(pages):
        if page + 1 < pages:
            project(page + 1)
        raw = raw_ref[page]
        unit = raw * inverse_norm(raw)
        unit_ref[page] = jnp.where(iota(unit.shape, 1) < length[page], unit, unit[:, 0:1]).T.astype(BF16)
        unit_copy(page).start()
        unit = unit.astype(BF16)
        table = jnp.concatenate([unit[:, part * 256:(part + 1) * 256] for part in range(parts)], axis=0)

        for tile in range(tiles):
            index = index_ref[page, tile:tile + 1, :]
            found = jnp.dot(table, one_hot(index & 255), preferred_element_type=F32)
            which = index >> 8
            chosen = found[0:dim]
            for part in range(1, parts):
                chosen = jnp.where(which == part, found[part * dim:(part + 1) * dim], chosen)
            chosen_ref[page, tile] = chosen.astype(BF16)
            if (tile + 1) % (tiles // 2) == 0:
                chosen_copy(page, tile // (tiles // 2)).start()
    index_copy.wait()
    for page in range(pages):
        raw_copy(page).wait()
        unit_copy(page).wait()
        for part in range(2):
            chosen_copy(page, part).wait()


def best_scores(queries, unit_ref, out, row):
    for page in range(unit_ref.shape[0]):
        scores = jnp.dot(unit_ref[page], queries, preferred_element_type=F32)
        top = jnp.max(scores.reshape(-1, 8, scores.shape[1]), axis=0)
        out[page, pl.ds(row, 1), :] = jnp.max(top, axis=0, keepdims=True)


def near_kernel(query_ref, unit_ref, hidden_any, best_ref, hidden_ref, arrived):
    hidden_copy = pltpu.make_async_copy(hidden_any, hidden_ref, arrived)
    hidden_copy.start()

    for tile in range(query_ref.shape[0]):
        best_scores(query_ref[tile], unit_ref, best_ref, tile)
    hidden_copy.wait()


def mixed(expo_ref, chosen_ref, tile):
    result = expo_ref[0, pl.ds(tile, 1), :] * chosen_ref[0, tile].astype(F32)
    for page in range(1, expo_ref.shape[0]):
        result = result + expo_ref[page, pl.ds(tile, 1), :] * chosen_ref[page, tile].astype(F32)
    return result


def far_kernel(multiplier, place_ref, query_ref, unit_ref, near_ref, chosen_ref, expo_ref, total_ref, pair_ref, best):
    core = place_ref[0]
    pages, chips = near_ref.shape[:2]
    dim, lanes = query_ref.shape[1:]
    near = pl.multiple_of(core * chips, chips)
    far = pl.multiple_of((1 - core) * chips, chips)
    for page in range(pages):
        best[page, pl.ds(near, chips), :] = near_ref[page]

    for tile in range(chips):
        best_scores(query_ref[tile], unit_ref, best, far + tile)

    segment = jnp.where(iota((lanes, lanes), 0) // 32 == iota((lanes, lanes), 1) // 32, 1.0, 0.0).astype(BF16)
    value = best[...].reshape(pages * 2 * chips, lanes)
    score = jnp.zeros_like(value)
    for _ in range(3):
        part = value.astype(BF16)
        score = score + jnp.dot(part, segment, preferred_element_type=F32)
        value = value - part.astype(F32)
    expo = jnp.exp(score * multiplier).reshape(pages, 2 * chips, lanes)
    expo_ref[...] = expo
    total = jnp.sum(expo, axis=0)
    total = jnp.where(iota((2 * chips, 128), 1) % 32 < 16, total[:, :128], total[:, 128:])
    total_ref[...] = total
    high = total.astype(BF16)
    low = (total - high.astype(F32)).astype(BF16)

    def one_mix(tile, carry):
        pair_ref[tile, 0:dim, :] = mixed(expo_ref, chosen_ref, far + tile).astype(BF16)
        pair_ref[tile, dim:dim + 16, 0:128] = high
        pair_ref[tile, dim:dim + 16, 128:256] = low
        return carry

    lax.fori_loop(0, chips, one_mix, 0, unroll=2)


def keep_kernel(place_ref, expo_ref, chosen_ref, keep_ref, target_ref):
    core, chip = place_ref[0], place_ref[1]
    chips, dim, lanes = keep_ref.shape
    near = core * chips

    def one_mix(tile, carry):
        keep_ref[tile] = mixed(expo_ref, chosen_ref, near + tile)
        return carry

    lax.fori_loop(0, chips, one_mix, 0, unroll=2)
    picked = jnp.zeros((dim, lanes), F32)
    for page in range(expo_ref.shape[0]):
        picked = jnp.where(iota((dim, lanes), 1) // 64 == page, chosen_ref[page, near + chip].astype(F32), picked)
    target_ref[...] = picked


def add_kernel(place_ref, keep_ref, total_ref, pair_ref, send_ref, own_ref):
    chips, dim, _ = keep_ref.shape
    total = total_ref[...] + (pair_ref[0, dim:dim + 16, 0:128].astype(F32) + pair_ref[0, dim:dim + 16, 128:256].astype(F32))
    high = total.astype(BF16)
    low = (total - high.astype(F32)).astype(BF16)
    for tile in range(chips):
        send_ref[tile, 0:dim, :] = (keep_ref[tile] + pair_ref[tile, 0:dim, :].astype(F32)).astype(BF16)
        send_ref[tile, dim:dim + 16, 0:128] = high
        send_ref[tile, dim:dim + 16, 128:256] = low
    chip = place_ref[1]
    own_ref[...] = keep_ref[chip] + pair_ref[chip, 0:dim, :].astype(F32)


def gradient_kernel(multiplier, place_ref, index_ref, expo_ref, received_ref, own_ref, target_ref, near_ref, far_ref, page_raw,
                    hidden, query_raw_ref, query_hidden, keep_ref, give_ref, query_grad_ref, inverse_total, score_grad, summed_grad,
                    accumulated, turned):
    core, chip = place_ref[0], place_ref[1]
    chips, dim, lanes = near_ref.shape
    tiles = 2 * chips
    mine = core * chips + chip
    pages, slots, _ = hidden.shape
    parts = slots // 256
    total = jnp.zeros((tiles, 128), F32)
    for source in range(chips):
        total = total + received_ref[source, dim:dim + 16, 0:128].astype(F32) + received_ref[source, dim:dim + 16, 128:256].astype(F32)
    inverse = 1.0 / total
    first = iota((tiles, 128), 1) % 32 < 16
    inverse_total[:, 0:128] = jnp.where(first, inverse, pltpu.roll(inverse, 16, 1))
    inverse_total[:, 128:256] = jnp.where(first, pltpu.roll(inverse, 112, 1), inverse)
    accumulated[...] = jnp.zeros_like(accumulated)

    def scattered(page, tile, weighted):
        index = index_ref[page, pl.ds(tile, 1), :]
        which = index >> 8
        left = jnp.concatenate([jnp.where(which == part, weighted, 0.0).astype(BF16) for part in range(parts)], axis=0)
        return lax.dot_general(left, one_hot(index & 255), NT, preferred_element_type=F32)

    for page in range(pages):
        is_target = (iota((tiles, lanes), 0) == mine) & (iota((tiles, lanes), 1) // 64 == page)
        score_grad[...] = (expo_ref[page] * inverse_total[...] - jnp.where(is_target, 1.0, 0.0)) * multiplier
        weighted = near_ref[chip].astype(F32) * score_grad[pl.ds(mine, 1), :]
        summed_grad[...] = scattered(page, mine, weighted - weighted.astype(BF16).astype(F32))
        for side, queries_ref in ((core, near_ref), (1 - core, far_ref)):
            for chip_of in range(chips):
                tile = side * chips + chip_of
                summed_grad[...] += scattered(page, tile, queries_ref[chip_of].astype(F32) * score_grad[pl.ds(tile, 1), :])
        grad = jnp.concatenate([summed_grad[part * dim:(part + 1) * dim] for part in range(parts)], axis=1)
        direction = unit_backward(grad, page_raw[page]).astype(BF16)
        accumulated[...] += jnp.dot(direction, hidden[page], preferred_element_type=F32)
    summed = own_ref[...]
    for source in range(chips):
        summed = summed + jnp.where(chip == source, 0.0, received_ref[source, 0:dim, :].astype(F32))
    query_grad = (summed * inverse_total[pl.ds(mine, 1), :] - target_ref[...]) * multiplier
    query_grad_ref[...] = query_grad.T
    direction = unit_backward(query_grad, query_raw_ref[...]).astype(BF16)
    turned[...] = (accumulated[...] + jnp.dot(direction, query_hidden[...], preferred_element_type=F32)).T
    half = keep_ref.shape[0]
    keep_ref[...] = turned[pl.ds(pl.multiple_of(core * half, half), half), :]
    give_ref[...] = turned[pl.ds(pl.multiple_of((1 - core) * half, half), half), :]


def shape(dims, kind):
    return jax.ShapeDtypeStruct(dims, kind)


def vmem(mib):
    return pltpu.CompilerParams(vmem_limit_bytes=mib * MIB)


def cost(flops, read):
    return pl.CostEstimate(flops=flops, bytes_accessed=read, transcendentals=0)


def swap_cores(value):
    return lax.ppermute(value, "core", [(0, 1), (1, 0)])


def summed(terms):
    return lax.optimization_barrier(jnp.sum(terms.astype(F32), axis=0)).astype(BF16)


def to_all(value, axis):
    return lax.all_to_all(jnp.broadcast_to(value[None], (lax.axis_size(axis),) + value.shape), axis, 0, 0, tiled=True)


def per_device(query_hidden, document_states, projection, lengths, best_token):
    query_count, tokens, hidden_size = query_hidden.shape
    pages, slots, _ = document_states.shape
    dim = projection.shape[1]
    chips, cores = lax.axis_size("chip"), lax.axis_size("core")
    tiles = chips * cores
    rows = query_count * tokens
    multiplier = 1.0 / (tokens * TEMPERATURE)
    smem = pl.BlockSpec(memory_space=pltpu.SMEM)
    inside = pl.BlockSpec(memory_space=pltpu.VMEM)
    anywhere = pl.BlockSpec(memory_space=pl.ANY)
    place = jnp.stack([lax.axis_index("core"), lax.axis_index("chip")]).astype(jnp.int32)
    query_rows = query_hidden.reshape(rows, hidden_size)

    query_raw, query_send = pl.pallas_call(
        query_kernel,
        in_specs=[anywhere] * 2,
        out_shape=(shape((dim, rows), F32), shape((chips, dim, rows), BF16)),
        scratch_shapes=[pltpu.VMEM((rows, hidden_size), BF16), pltpu.VMEM((hidden_size, dim), BF16), pltpu.SemaphoreType.DMA((2,))],
        compiler_params=vmem(QUERY_MIB),
        cost_estimate=cost(2 * rows * hidden_size * dim, 2 * MIB),
        name="query_project",
    )(query_rows, projection)
    near = lax.all_to_all(query_send, "chip", 0, 0, tiled=True)

    page_raw, page_unit, chosen, index = pl.pallas_call(
        page_kernel,
        in_specs=[anywhere] * 4,
        out_specs=[anywhere] * 4,
        out_shape=(
            shape((pages, dim, slots), F32),
            shape((pages, slots, dim), BF16),
            shape((pages, tiles, dim, rows), BF16),
            shape((pages, tiles, rows), jnp.int32),
        ),
        scratch_shapes=[
            pltpu.VMEM((pages, slots, hidden_size), BF16),
            pltpu.VMEM((hidden_size, dim), BF16),
            pltpu.VMEM((tokens, pages, chips * cores * query_count), jnp.int32),
            pltpu.SMEM((pages,), jnp.int32),
            pltpu.VMEM((128, 128), F32),
            pltpu.VMEM((pages, dim, slots), F32),
            pltpu.VMEM((pages, slots, dim), BF16),
            pltpu.VMEM((pages, tiles, dim, rows), BF16),
            pltpu.VMEM((pages, tiles, rows), jnp.int32),
            pltpu.SemaphoreType.DMA((pages + 4,)),
            pltpu.SemaphoreType.DMA((4, pages)),
            pltpu.SemaphoreType.DMA,
        ],
        compiler_params=vmem(PAGE_MIB),
        cost_estimate=cost(2 * pages * slots * dim * (hidden_size + tiles * rows), 16 * MIB),
        name="page_project",
    )(lengths, document_states, projection, jnp.transpose(best_token, (1, 2, 0)))

    near, index = lax.optimization_barrier((near, index))
    far = swap_cores(near)
    near_best, page_hidden = pl.pallas_call(
        near_kernel,
        in_specs=[inside] * 2 + [anywhere],
        out_shape=(shape((pages, chips, rows), F32), shape((pages, slots, hidden_size), BF16)),
        scratch_shapes=[pltpu.SemaphoreType.DMA],
        compiler_params=vmem(NEAR_MIB),
        cost_estimate=cost(pages * slots * dim * tiles * rows, 2 * MIB),
        name="near_scores",
    )(near, page_unit, document_states)
    expo, total, pair = pl.pallas_call(
        lambda *refs: far_kernel(multiplier, *refs),
        in_specs=[smem] + [inside] * 4,
        out_shape=(shape((pages, tiles, rows), F32), shape((tiles, 128), F32), shape((chips, dim + 16, rows), BF16)),
        scratch_shapes=[pltpu.VMEM((pages, tiles, rows), F32)],
        compiler_params=vmem(FAR_MIB),
        cost_estimate=cost(pages * slots * dim * tiles * rows, 8 * MIB),
        name="far_scores",
    )(place, far, page_unit, near_best, chosen)
    keep, target = pl.pallas_call(
        keep_kernel,
        in_specs=[smem] + [inside] * 2,
        out_shape=(shape((chips, dim, rows), F32), shape((dim, rows), F32)),
        compiler_params=vmem(24),
        cost_estimate=cost(2 * pages * dim * tiles * rows, 4 * MIB),
        name="keep_terms",
    )(place, expo, chosen)
    send, own = pl.pallas_call(
        add_kernel,
        in_specs=[smem] + [inside] * 3,
        out_shape=(shape((chips, dim + 16, rows), BF16), shape((dim, rows), F32)),
        compiler_params=vmem(8),
        name="add_pair",
    )(place, keep, total, swap_cores(pair))
    received = lax.all_to_all(send, "chip", 0, 0, tiled=True)

    half = hidden_size // cores
    weight_keep, weight_give, query_grad = pl.pallas_call(
        lambda *refs: gradient_kernel(multiplier, *refs),
        in_specs=[smem] + [inside] * 11,
        out_shape=(shape((half, dim), F32), shape((half, dim), F32), shape((rows, dim), F32)),
        scratch_shapes=[
            pltpu.VMEM((tiles, rows), F32),
            pltpu.VMEM((tiles, rows), F32),
            pltpu.VMEM((slots // 256 * dim, 256), F32),
            pltpu.VMEM((dim, hidden_size), F32),
            pltpu.VMEM((hidden_size, dim), F32),
        ],
        compiler_params=vmem(GRADIENT_MIB),
        cost_estimate=cost(2 * pages * slots * dim * (hidden_size + tiles * rows), 16 * MIB),
        name="gradients",
    )(place, index, expo, received, own, target, near, far, page_raw, page_hidden, query_raw, query_rows)

    halves = (weight_keep + swap_cores(weight_give)).astype(BF16)
    chunk = summed(lax.all_to_all(halves.reshape(chips, half // chips, dim), "chip", 0, 0, tiled=True))
    chunk = summed(to_all(chunk, "dp"))
    mine = to_all(chunk, "chip").reshape(half, dim)
    other = swap_cores(mine)
    first = lax.axis_index("core") == 0
    weight_grad = jnp.concatenate([jnp.where(first, mine, other), jnp.where(first, other, mine)], axis=0).astype(F32)
    return (weight_grad, query_grad.reshape(query_count, tokens, dim))


def solution(mesh):
    groups, gallery = mesh.devices.shape
    levels = Mesh(mesh.devices.reshape(groups, gallery // 2, 2), ("dp", "chip", "core"))
    every = ("dp", "chip", "core")
    return jax.shard_map(
        per_device,
        mesh=levels,
        in_specs=(P(every, None, None), P(every, None, None), P(), P(every), P("dp", None, ("chip", "core"))),
        out_specs=(P(), P(every, None, None)),
        check_vma=False,
    )
```

```python
import jax
import jax.numpy as jnp
from jax import lax
from jax.experimental import pallas as pl
from jax.experimental.pallas import tpu as pltpu
from jax.sharding import Mesh, PartitionSpec as P

F32 = jnp.float32
BF16 = jnp.bfloat16
EPSILON = 1e-06
TEMPERATURE = 0.02
MIB = 1024 * 1024
QUERY_MIB, PAGE_MIB, NEAR_MIB, FAR_MIB, GRADIENT_MIB = 60, 56, 40, 24, 14

NT = (((1,), (1,)), ((), ()))


def inverse_norm(raw):
    value = jnp.sum(raw * raw, axis=0, keepdims=True) + EPSILON
    guess = lax.rsqrt(value)
    return guess * (1.5 - 0.5 * value * guess * guess)


def unit_backward(grad_unit, raw):
    inverse = inverse_norm(raw)
    unit = raw * inverse
    return (grad_unit - unit * jnp.sum(unit * grad_unit, axis=0, keepdims=True)) * inverse


def iota(shape, axis):
    return lax.broadcasted_iota(jnp.int32, shape, axis)


def one_hot(low):
    index = low.astype(F32).astype(BF16)
    positions = iota((256, low.shape[1]), 0).astype(F32).astype(BF16)
    return jnp.where(positions == index, jnp.ones((), BF16), jnp.zeros((), BF16))


def query_kernel(hidden_any, weight_any, raw_ref, send_ref, hidden, weight, arrived):
    copies = [
        pltpu.make_async_copy(weight_any, weight, arrived.at[0]),
        pltpu.make_async_copy(hidden_any, hidden, arrived.at[1]),
    ]
    for copy in copies:
        copy.start()
    for copy in copies:
        copy.wait()
    raw = jnp.dot(hidden[...], weight[...], preferred_element_type=F32).T
    raw_ref[...] = raw
    unit = (raw * inverse_norm(raw)).astype(BF16)
    for block in range(send_ref.shape[0]):
        send_ref[block] = unit


def page_kernel(length_any, hidden_any, weight_any, best_any, raw_any, unit_any, chosen_any, index_any,
                hidden, weight, best, length, turned, raw_ref, unit_ref, chosen_ref, index_ref, arrived, left, index_left):
    pages, slots, _ = hidden.shape
    dim, tiles = weight.shape[1], index_ref.shape[1]
    parts = slots // 256
    small = [
        pltpu.make_async_copy(best_any, best, arrived.at[pages]),
        pltpu.make_async_copy(weight_any, weight, arrived.at[pages + 1]),
        pltpu.make_async_copy(length_any, length, arrived.at[pages + 2]),
    ]

    def page_copy(page):
        return pltpu.make_async_copy(hidden_any.at[page], hidden.at[page], arrived.at[page])

    def first_copy(part):
        some = pl.ds(part * slots // 2, slots // 2)
        return pltpu.make_async_copy(hidden_any.at[0, some], hidden.at[0, some], arrived.at[pages + 2 + part if part else 0])

    def raw_copy(page):
        return pltpu.make_async_copy(raw_ref.at[page], raw_any.at[page], left.at[0, page])

    def unit_copy(page):
        return pltpu.make_async_copy(unit_ref.at[page], unit_any.at[page], left.at[1, page])

    def chosen_copy(page, part):
        some = pl.ds(part * (tiles // 2), tiles // 2)
        return pltpu.make_async_copy(chosen_ref.at[page, some], chosen_any.at[page, some], left.at[2 + part, page])

    first_copy(0).start()
    for copy in small:
        copy.start()
    first_copy(1).start()
    page_copy(1).start()
    small[0].wait()
    for page in range(pages):
        tokens = best[:, page, :].astype(F32)
        turned[...] = jnp.concatenate([tokens, jnp.zeros((96, 128), F32)], axis=0).T
        for core in range(2):
            halves = []
            for half in range(2):
                row = jnp.zeros((8, 128), F32)
                for query in range(4):
                    piece = turned[pl.ds(core * 8 + half * 4 + query, 8, stride=16), :]
                    row = row + (pltpu.roll(piece, 32 * query, 1) if query else piece)
                halves.append(row)
            index_ref[page, core * 8:core * 8 + 8, :] = jnp.concatenate(halves, axis=1).astype(jnp.int32)
    index_copy = pltpu.make_async_copy(index_ref, index_any, index_left)
    index_copy.start()
    small[1].wait()
    small[2].wait()

    def project(page):
        if page + 2 < pages:
            page_copy(page + 2).start()
        if page:
            page_copy(page).wait()
            raw_ref[page] = jnp.dot(hidden[page], weight[...], preferred_element_type=F32).T
        else:
            for part in range(2):
                some = slice(part * slots // 2, (part + 1) * slots // 2)
                first_copy(part).wait()
                raw_ref[0, :, some] = jnp.dot(hidden[0, some], weight[...], preferred_element_type=F32).T
        raw_copy(page).start()

    project(0)
    for page in range(pages):
        if page + 1 < pages:
            project(page + 1)
        raw = raw_ref[page]
        unit = raw * inverse_norm(raw)
        unit_ref[page] = jnp.where(iota(unit.shape, 1) < length[page], unit, unit[:, 0:1]).T.astype(BF16)
        unit_copy(page).start()
        unit = unit.astype(BF16)
        table = jnp.concatenate([unit[:, part * 256:(part + 1) * 256] for part in range(parts)], axis=0)

        for tile in range(tiles):
            index = index_ref[page, tile:tile + 1, :]
            found = jnp.dot(table, one_hot(index & 255), preferred_element_type=F32)
            which = index >> 8
            chosen = found[0:dim]
            for part in range(1, parts):
                chosen = jnp.where(which == part, found[part * dim:(part + 1) * dim], chosen)
            chosen_ref[page, tile] = chosen.astype(BF16)
            if (tile + 1) % (tiles // 2) == 0:
                chosen_copy(page, tile // (tiles // 2)).start()
    index_copy.wait()
    for page in range(pages):
        raw_copy(page).wait()
        unit_copy(page).wait()
        for part in range(2):
            chosen_copy(page, part).wait()


def best_scores(queries, unit_ref, out, row):
    for page in range(unit_ref.shape[0]):
        scores = jnp.dot(unit_ref[page], queries, preferred_element_type=F32)
        top = jnp.max(scores.reshape(-1, 8, scores.shape[1]), axis=0)
        out[page, pl.ds(row, 1), :] = jnp.max(top, axis=0, keepdims=True)


def near_kernel(query_ref, unit_ref, hidden_any, best_ref, hidden_ref, arrived):
    hidden_copy = pltpu.make_async_copy(hidden_any, hidden_ref, arrived)
    hidden_copy.start()

    for tile in range(query_ref.shape[0]):
        best_scores(query_ref[tile], unit_ref, best_ref, tile)
    hidden_copy.wait()


def mixed(expo_ref, chosen_ref, tile):
    result = expo_ref[0, pl.ds(tile, 1), :] * chosen_ref[0, tile].astype(F32)
    for page in range(1, expo_ref.shape[0]):
        result = result + expo_ref[page, pl.ds(tile, 1), :] * chosen_ref[page, tile].astype(F32)
    return result


def far_kernel(multiplier, place_ref, query_ref, unit_ref, near_ref, chosen_ref, expo_ref, total_ref, pair_ref, best):
    core = place_ref[0]
    pages, chips = near_ref.shape[:2]
    dim, lanes = query_ref.shape[1:]
    near = pl.multiple_of(core * chips, chips)
    far = pl.multiple_of((1 - core) * chips, chips)
    for page in range(pages):
        best[page, pl.ds(near, chips), :] = near_ref[page]

    for tile in range(chips):
        best_scores(query_ref[tile], unit_ref, best, far + tile)

    segment = jnp.where(iota((lanes, lanes), 0) // 32 == iota((lanes, lanes), 1) // 32, 1.0, 0.0).astype(BF16)
    value = best[...].reshape(pages * 2 * chips, lanes)
    score = jnp.zeros_like(value)
    for _ in range(3):
        part = value.astype(BF16)
        score = score + jnp.dot(part, segment, preferred_element_type=F32)
        value = value - part.astype(F32)
    expo = jnp.exp(score * multiplier).reshape(pages, 2 * chips, lanes)
    expo_ref[...] = expo
    total = jnp.sum(expo, axis=0)
    total = jnp.where(iota((2 * chips, 128), 1) % 32 < 16, total[:, :128], total[:, 128:])
    total_ref[...] = total
    high = total.astype(BF16)
    low = (total - high.astype(F32)).astype(BF16)

    def one_mix(tile, carry):
        pair_ref[tile, 0:dim, :] = mixed(expo_ref, chosen_ref, far + tile).astype(BF16)
        pair_ref[tile, dim:dim + 16, 0:128] = high
        pair_ref[tile, dim:dim + 16, 128:256] = low
        return carry

    lax.fori_loop(0, chips, one_mix, 0, unroll=2)


def keep_kernel(place_ref, expo_ref, chosen_ref, keep_ref, target_ref):
    core, chip = place_ref[0], place_ref[1]
    chips, dim, lanes = keep_ref.shape
    near = core * chips

    def one_mix(tile, carry):
        keep_ref[tile] = mixed(expo_ref, chosen_ref, near + tile)
        return carry

    lax.fori_loop(0, chips, one_mix, 0, unroll=2)
    picked = jnp.zeros((dim, lanes), F32)
    for page in range(expo_ref.shape[0]):
        picked = jnp.where(iota((dim, lanes), 1) // 64 == page, chosen_ref[page, near + chip].astype(F32), picked)
    target_ref[...] = picked


def add_kernel(place_ref, keep_ref, total_ref, pair_ref, send_ref, own_ref):
    chips, dim, _ = keep_ref.shape
    total = total_ref[...] + (pair_ref[0, dim:dim + 16, 0:128].astype(F32) + pair_ref[0, dim:dim + 16, 128:256].astype(F32))
    high = total.astype(BF16)
    low = (total - high.astype(F32)).astype(BF16)
    for tile in range(chips):
        send_ref[tile, 0:dim, :] = (keep_ref[tile] + pair_ref[tile, 0:dim, :].astype(F32)).astype(BF16)
        send_ref[tile, dim:dim + 16, 0:128] = high
        send_ref[tile, dim:dim + 16, 128:256] = low
    chip = place_ref[1]
    own_ref[...] = keep_ref[chip] + pair_ref[chip, 0:dim, :].astype(F32)


def gradient_kernel(multiplier, place_ref, index_ref, expo_ref, received_ref, own_ref, target_ref, near_ref, far_ref, page_raw,
                    hidden, query_raw_ref, query_hidden, give_ref, query_grad_ref, page_direction_ref, query_direction_ref,
                    inverse_total, score_grad, summed_grad):
    core, chip = place_ref[0], place_ref[1]
    chips, dim, lanes = near_ref.shape
    tiles = 2 * chips
    mine = core * chips + chip
    pages, slots, _ = hidden.shape
    parts = slots // 256
    total = jnp.zeros((tiles, 128), F32)
    for source in range(chips):
        total = total + received_ref[source, dim:dim + 16, 0:128].astype(F32) + received_ref[source, dim:dim + 16, 128:256].astype(F32)
    inverse = 1.0 / total
    first = iota((tiles, 128), 1) % 32 < 16
    inverse_total[:, 0:128] = jnp.where(first, inverse, pltpu.roll(inverse, 16, 1))
    inverse_total[:, 128:256] = jnp.where(first, pltpu.roll(inverse, 112, 1), inverse)
    half = give_ref.shape[0]
    columns = pl.ds(pl.multiple_of((1 - core) * half, half), half)

    def scattered(page, tile, weighted):
        index = index_ref[page, pl.ds(tile, 1), :]
        which = index >> 8
        left = jnp.concatenate([jnp.where(which == part, weighted, 0.0).astype(BF16) for part in range(parts)], axis=0)
        return lax.dot_general(left, one_hot(index & 255), NT, preferred_element_type=F32)

    for page in range(pages):
        is_target = (iota((tiles, lanes), 0) == mine) & (iota((tiles, lanes), 1) // 64 == page)
        score_grad[...] = (expo_ref[page] * inverse_total[...] - jnp.where(is_target, 1.0, 0.0)) * multiplier
        weighted = near_ref[chip].astype(F32) * score_grad[pl.ds(mine, 1), :]
        summed_grad[...] = scattered(page, mine, weighted - weighted.astype(BF16).astype(F32))
        for side, queries_ref in ((core, near_ref), (1 - core, far_ref)):
            for chip_of in range(chips):
                tile = side * chips + chip_of
                summed_grad[...] += scattered(page, tile, queries_ref[chip_of].astype(F32) * score_grad[pl.ds(tile, 1), :])
        grad = jnp.concatenate([summed_grad[part * dim:(part + 1) * dim] for part in range(parts)], axis=1)
        direction = unit_backward(grad, page_raw[page]).astype(BF16)
        page_direction_ref[page] = direction
    summed = own_ref[...]
    for source in range(chips):
        summed = summed + jnp.where(chip == source, 0.0, received_ref[source, 0:dim, :].astype(F32))
    query_grad = (summed * inverse_total[pl.ds(mine, 1), :] - target_ref[...]) * multiplier
    query_grad_ref[...] = query_grad.T
    direction = unit_backward(query_grad, query_raw_ref[...]).astype(BF16)
    query_direction_ref[...] = direction
    grad = jnp.dot(direction, query_hidden[:, columns], preferred_element_type=F32)
    for page in range(pages):
        grad = grad + jnp.dot(page_direction_ref[page], hidden[page, :, columns], preferred_element_type=F32)
    give_ref[...] = grad.T


def weight_keep_kernel(place_ref, page_direction_ref, query_direction_ref, hidden, query_hidden, keep_ref):
    half = keep_ref.shape[0]
    columns = pl.ds(pl.multiple_of(place_ref[0] * half, half), half)
    grad = jnp.dot(query_direction_ref[...], query_hidden[:, columns], preferred_element_type=F32)
    for page in range(hidden.shape[0]):
        grad = grad + jnp.dot(page_direction_ref[page], hidden[page, :, columns], preferred_element_type=F32)
    keep_ref[...] = grad.T


def shape(dims, kind):
    return jax.ShapeDtypeStruct(dims, kind)


def vmem(mib):
    return pltpu.CompilerParams(vmem_limit_bytes=mib * MIB)


def cost(flops, read):
    return pl.CostEstimate(flops=flops, bytes_accessed=read, transcendentals=0)


def swap_cores(value):
    return lax.ppermute(value, "core", [(0, 1), (1, 0)])


def summed(terms):
    return lax.optimization_barrier(jnp.sum(terms.astype(F32), axis=0)).astype(BF16)


def to_all(value, axis):
    return lax.all_to_all(jnp.broadcast_to(value[None], (lax.axis_size(axis),) + value.shape), axis, 0, 0, tiled=True)


def per_device(query_hidden, document_states, projection, lengths, best_token):
    query_count, tokens, hidden_size = query_hidden.shape
    pages, slots, _ = document_states.shape
    dim = projection.shape[1]
    chips, cores = lax.axis_size("chip"), lax.axis_size("core")
    tiles = chips * cores
    rows = query_count * tokens
    multiplier = 1.0 / (tokens * TEMPERATURE)
    smem = pl.BlockSpec(memory_space=pltpu.SMEM)
    inside = pl.BlockSpec(memory_space=pltpu.VMEM)
    anywhere = pl.BlockSpec(memory_space=pl.ANY)
    place = jnp.stack([lax.axis_index("core"), lax.axis_index("chip")]).astype(jnp.int32)
    query_rows = query_hidden.reshape(rows, hidden_size)

    query_raw, query_send = pl.pallas_call(
        query_kernel,
        in_specs=[anywhere] * 2,
        out_shape=(shape((dim, rows), F32), shape((chips, dim, rows), BF16)),
        scratch_shapes=[pltpu.VMEM((rows, hidden_size), BF16), pltpu.VMEM((hidden_size, dim), BF16), pltpu.SemaphoreType.DMA((2,))],
        compiler_params=vmem(QUERY_MIB),
        cost_estimate=cost(2 * rows * hidden_size * dim, 2 * MIB),
        name="query_project",
    )(query_rows, projection)
    near = lax.all_to_all(query_send, "chip", 0, 0, tiled=True)

    page_raw, page_unit, chosen, index = pl.pallas_call(
        page_kernel,
        in_specs=[anywhere] * 4,
        out_specs=[anywhere] * 4,
        out_shape=(
            shape((pages, dim, slots), F32),
            shape((pages, slots, dim), BF16),
            shape((pages, tiles, dim, rows), BF16),
            shape((pages, tiles, rows), jnp.int32),
        ),
        scratch_shapes=[
            pltpu.VMEM((pages, slots, hidden_size), BF16),
            pltpu.VMEM((hidden_size, dim), BF16),
            pltpu.VMEM((tokens, pages, chips * cores * query_count), jnp.int32),
            pltpu.SMEM((pages,), jnp.int32),
            pltpu.VMEM((128, 128), F32),
            pltpu.VMEM((pages, dim, slots), F32),
            pltpu.VMEM((pages, slots, dim), BF16),
            pltpu.VMEM((pages, tiles, dim, rows), BF16),
            pltpu.VMEM((pages, tiles, rows), jnp.int32),
            pltpu.SemaphoreType.DMA((pages + 4,)),
            pltpu.SemaphoreType.DMA((4, pages)),
            pltpu.SemaphoreType.DMA,
        ],
        compiler_params=vmem(PAGE_MIB),
        cost_estimate=cost(2 * pages * slots * dim * (hidden_size + tiles * rows), 16 * MIB),
        name="page_project",
    )(lengths, document_states, projection, jnp.transpose(best_token, (1, 2, 0)))

    near, index = lax.optimization_barrier((near, index))
    far = swap_cores(near)
    near_best, page_hidden = pl.pallas_call(
        near_kernel,
        in_specs=[inside] * 2 + [anywhere],
        out_shape=(shape((pages, chips, rows), F32), shape((pages, slots, hidden_size), BF16)),
        scratch_shapes=[pltpu.SemaphoreType.DMA],
        compiler_params=vmem(NEAR_MIB),
        cost_estimate=cost(pages * slots * dim * tiles * rows, 2 * MIB),
        name="near_scores",
    )(near, page_unit, document_states)
    expo, total, pair = pl.pallas_call(
        lambda *refs: far_kernel(multiplier, *refs),
        in_specs=[smem] + [inside] * 4,
        out_shape=(shape((pages, tiles, rows), F32), shape((tiles, 128), F32), shape((chips, dim + 16, rows), BF16)),
        scratch_shapes=[pltpu.VMEM((pages, tiles, rows), F32)],
        compiler_params=vmem(FAR_MIB),
        cost_estimate=cost(pages * slots * dim * tiles * rows, 8 * MIB),
        name="far_scores",
    )(place, far, page_unit, near_best, chosen)
    keep, target = pl.pallas_call(
        keep_kernel,
        in_specs=[smem] + [inside] * 2,
        out_shape=(shape((chips, dim, rows), F32), shape((dim, rows), F32)),
        compiler_params=vmem(24),
        cost_estimate=cost(2 * pages * dim * tiles * rows, 4 * MIB),
        name="keep_terms",
    )(place, expo, chosen)
    send, own = pl.pallas_call(
        add_kernel,
        in_specs=[smem] + [inside] * 3,
        out_shape=(shape((chips, dim + 16, rows), BF16), shape((dim, rows), F32)),
        compiler_params=vmem(8),
        name="add_pair",
    )(place, keep, total, swap_cores(pair))
    received = lax.all_to_all(send, "chip", 0, 0, tiled=True)

    half = hidden_size // cores
    weight_give, query_grad, page_direction, query_direction = pl.pallas_call(
        lambda *refs: gradient_kernel(multiplier, *refs),
        in_specs=[smem] + [inside] * 11,
        out_shape=(
            shape((half, dim), F32),
            shape((rows, dim), F32),
            shape((pages, dim, slots), BF16),
            shape((dim, rows), BF16),
        ),
        scratch_shapes=[
            pltpu.VMEM((tiles, rows), F32),
            pltpu.VMEM((tiles, rows), F32),
            pltpu.VMEM((slots // 256 * dim, 256), F32),
        ],
        compiler_params=vmem(GRADIENT_MIB),
        cost_estimate=cost(2 * pages * slots * dim * (hidden_size + tiles * rows), 16 * MIB),
        name="gradients",
    )(place, index, expo, received, own, target, near, far, page_raw, page_hidden, query_raw, query_rows)

    weight_keep = pl.pallas_call(
        weight_keep_kernel,
        in_specs=[smem] + [inside] * 4,
        out_shape=shape((half, dim), F32),
        compiler_params=vmem(GRADIENT_MIB),
        cost_estimate=cost(pages * slots * dim * hidden_size, 6 * MIB),
        name="weight_keep",
    )(place, page_direction, query_direction, page_hidden, query_rows)

    halves = (weight_keep + swap_cores(weight_give)).astype(BF16)
    chunk = summed(lax.all_to_all(halves.reshape(chips, half // chips, dim), "chip", 0, 0, tiled=True))
    chunk = summed(to_all(chunk, "dp"))
    mine = to_all(chunk, "chip").reshape(half, dim)
    other = swap_cores(mine)
    first = lax.axis_index("core") == 0
    weight_grad = jnp.concatenate([jnp.where(first, mine, other), jnp.where(first, other, mine)], axis=0).astype(F32)
    return (weight_grad, query_grad.reshape(query_count, tokens, dim))


def solution(mesh):
    groups, gallery = mesh.devices.shape
    levels = Mesh(mesh.devices.reshape(groups, gallery // 2, 2), ("dp", "chip", "core"))
    every = ("dp", "chip", "core")
    return jax.shard_map(
        per_device,
        mesh=levels,
        in_specs=(P(every, None, None), P(every, None, None), P(), P(every), P("dp", None, ("chip", "core"))),
        out_specs=(P(), P(every, None, None)),
        check_vma=False,
    )
```

```python
import jax
import jax.numpy as jnp
from jax import lax
from jax.experimental import pallas as pl
from jax.experimental.pallas import tpu as pltpu
from jax.sharding import Mesh, PartitionSpec as P

F32 = jnp.float32
BF16 = jnp.bfloat16
EPSILON = 1e-06
TEMPERATURE = 0.02
MIB = 1024 * 1024
QUERY_MIB, PAGE_MIB, NEAR_MIB, FAR_MIB, GRADIENT_MIB = 60, 56, 40, 24, 14

NT = (((1,), (1,)), ((), ()))


def inverse_norm(raw):
    value = jnp.sum(raw * raw, axis=0, keepdims=True) + EPSILON
    guess = lax.rsqrt(value)
    return guess * (1.5 - 0.5 * value * guess * guess)


def unit_backward(grad_unit, raw):
    inverse = inverse_norm(raw)
    unit = raw * inverse
    return (grad_unit - unit * jnp.sum(unit * grad_unit, axis=0, keepdims=True)) * inverse


def iota(shape, axis):
    return lax.broadcasted_iota(jnp.int32, shape, axis)


def one_hot(low):
    index = low.astype(F32).astype(BF16)
    positions = iota((256, low.shape[1]), 0).astype(F32).astype(BF16)
    return jnp.where(positions == index, jnp.ones((), BF16), jnp.zeros((), BF16))


def query_kernel(hidden_any, weight_any, raw_ref, send_ref, hidden, weight, arrived):
    copies = [
        pltpu.make_async_copy(weight_any, weight, arrived.at[0]),
        pltpu.make_async_copy(hidden_any, hidden, arrived.at[1]),
    ]
    for copy in copies:
        copy.start()
    for copy in copies:
        copy.wait()
    raw = jnp.dot(hidden[...], weight[...], preferred_element_type=F32).T
    raw_ref[...] = raw
    unit = (raw * inverse_norm(raw)).astype(BF16)
    for block in range(send_ref.shape[0]):
        send_ref[block] = unit


def page_kernel(length_any, hidden_any, weight_any, best_any, raw_any, unit_any, chosen_any, index_any,
                hidden, weight, best, length, turned, raw_ref, unit_ref, chosen_ref, index_ref, arrived, left, index_left):
    pages, slots, _ = hidden.shape
    dim, tiles = weight.shape[1], index_ref.shape[1]
    parts = slots // 256
    small = [
        pltpu.make_async_copy(best_any, best, arrived.at[pages]),
        pltpu.make_async_copy(weight_any, weight, arrived.at[pages + 1]),
        pltpu.make_async_copy(length_any, length, arrived.at[pages + 2]),
    ]

    def page_copy(page):
        return pltpu.make_async_copy(hidden_any.at[page], hidden.at[page], arrived.at[page])

    def first_copy(part):
        some = pl.ds(part * slots // 2, slots // 2)
        return pltpu.make_async_copy(hidden_any.at[0, some], hidden.at[0, some], arrived.at[pages + 2 + part if part else 0])

    def raw_copy(page):
        return pltpu.make_async_copy(raw_ref.at[page], raw_any.at[page], left.at[0, page])

    def unit_copy(page):
        return pltpu.make_async_copy(unit_ref.at[page], unit_any.at[page], left.at[1, page])

    def chosen_copy(page, part):
        some = pl.ds(part * (tiles // 2), tiles // 2)
        return pltpu.make_async_copy(chosen_ref.at[page, some], chosen_any.at[page, some], left.at[2 + part, page])

    first_copy(0).start()
    for copy in small:
        copy.start()
    first_copy(1).start()
    page_copy(1).start()
    small[0].wait()
    for page in range(pages):
        tokens = best[:, page, :].astype(F32)
        turned[...] = jnp.concatenate([tokens, jnp.zeros((96, 128), F32)], axis=0).T
        for core in range(2):
            halves = []
            for half in range(2):
                row = jnp.zeros((8, 128), F32)
                for query in range(4):
                    piece = turned[pl.ds(core * 8 + half * 4 + query, 8, stride=16), :]
                    row = row + (pltpu.roll(piece, 32 * query, 1) if query else piece)
                halves.append(row)
            index_ref[page, core * 8:core * 8 + 8, :] = jnp.concatenate(halves, axis=1).astype(jnp.int32)
    index_copy = pltpu.make_async_copy(index_ref, index_any, index_left)
    index_copy.start()
    small[1].wait()
    small[2].wait()

    def project(page):
        if page + 2 < pages:
            page_copy(page + 2).start()
        if page:
            page_copy(page).wait()
            raw_ref[page] = jnp.dot(hidden[page], weight[...], preferred_element_type=F32).T
        else:
            for part in range(2):
                some = slice(part * slots // 2, (part + 1) * slots // 2)
                first_copy(part).wait()
                raw_ref[0, :, some] = jnp.dot(hidden[0, some], weight[...], preferred_element_type=F32).T
        raw_copy(page).start()

    project(0)
    for page in range(pages):
        if page + 1 < pages:
            project(page + 1)
        raw = raw_ref[page]
        unit = raw * inverse_norm(raw)
        unit_ref[page] = jnp.where(iota(unit.shape, 1) < length[page], unit, unit[:, 0:1]).T.astype(BF16)
        unit_copy(page).start()
        unit = unit.astype(BF16)
        table = jnp.concatenate([unit[:, part * 256:(part + 1) * 256] for part in range(parts)], axis=0)

        for tile in range(tiles):
            index = index_ref[page, tile:tile + 1, :]
            found = jnp.dot(table, one_hot(index & 255), preferred_element_type=F32)
            which = index >> 8
            chosen = found[0:dim]
            for part in range(1, parts):
                chosen = jnp.where(which == part, found[part * dim:(part + 1) * dim], chosen)
            chosen_ref[page, tile] = chosen.astype(BF16)
            if (tile + 1) % (tiles // 2) == 0:
                chosen_copy(page, tile // (tiles // 2)).start()
    index_copy.wait()
    for page in range(pages):
        raw_copy(page).wait()
        unit_copy(page).wait()
        for part in range(2):
            chosen_copy(page, part).wait()


def best_scores(queries, unit_ref, out, row):
    for page in range(unit_ref.shape[0]):
        scores = jnp.dot(unit_ref[page], queries, preferred_element_type=F32)
        top = jnp.max(scores.reshape(-1, 8, scores.shape[1]), axis=0)
        out[page, pl.ds(row, 1), :] = jnp.max(top, axis=0, keepdims=True)


def near_kernel(query_ref, unit_ref, hidden_any, best_ref, hidden_ref, arrived):
    hidden_copy = pltpu.make_async_copy(hidden_any, hidden_ref, arrived)
    hidden_copy.start()

    for tile in range(query_ref.shape[0]):
        best_scores(query_ref[tile], unit_ref, best_ref, tile)
    hidden_copy.wait()


def split_total(total):
    high = total.astype(BF16)
    rest = total - high.astype(F32)
    middle = rest.astype(BF16).astype(F32)
    return high, jnp.where(iota(total.shape, 1) % 16 < 8, middle, rest - middle).astype(BF16)


def joined_total(high, small):
    small = small.astype(F32)
    other = jnp.where(iota(small.shape, 1) % 16 < 8, pltpu.roll(small, 120, 1), pltpu.roll(small, 8, 1))
    return high.astype(F32) + (small + other)


def mixed(expo_ref, chosen_ref, tile):
    result = expo_ref[0, pl.ds(tile, 1), :] * chosen_ref[0, tile].astype(F32)
    for page in range(1, expo_ref.shape[0]):
        result = result + expo_ref[page, pl.ds(tile, 1), :] * chosen_ref[page, tile].astype(F32)
    return result


def far_kernel(multiplier, place_ref, query_ref, unit_ref, near_ref, chosen_ref, expo_ref, total_ref, pair_ref, best):
    core = place_ref[0]
    pages, chips = near_ref.shape[:2]
    dim, lanes = query_ref.shape[1:]
    near = pl.multiple_of(core * chips, chips)
    far = pl.multiple_of((1 - core) * chips, chips)
    for page in range(pages):
        best[page, pl.ds(near, chips), :] = near_ref[page]

    for tile in range(chips):
        best_scores(query_ref[tile], unit_ref, best, far + tile)

    segment = jnp.where(iota((lanes, lanes), 0) // 32 == iota((lanes, lanes), 1) // 32, 1.0, 0.0).astype(BF16)
    value = best[...].reshape(pages * 2 * chips, lanes)
    score = jnp.zeros_like(value)
    for _ in range(3):
        part = value.astype(BF16)
        score = score + jnp.dot(part, segment, preferred_element_type=F32)
        value = value - part.astype(F32)
    expo = jnp.exp(score * multiplier).reshape(pages, 2 * chips, lanes)
    expo_ref[...] = expo
    total = jnp.sum(expo, axis=0)
    total = jnp.where(iota((2 * chips, 128), 1) % 32 < 16, total[:, :128], total[:, 128:])
    total_ref[...] = total
    high, low = split_total(total)

    def one_mix(tile, carry):
        pair_ref[tile, 0:dim, :] = mixed(expo_ref, chosen_ref, far + tile).astype(BF16)
        pair_ref[tile, dim:dim + 16, 0:128] = high
        pair_ref[tile, dim:dim + 16, 128:256] = low
        return carry

    lax.fori_loop(0, chips, one_mix, 0, unroll=2)


def keep_kernel(place_ref, expo_ref, chosen_ref, keep_ref, target_ref):
    core, chip = place_ref[0], place_ref[1]
    chips, dim, lanes = keep_ref.shape
    near = core * chips

    def one_mix(tile, carry):
        keep_ref[tile] = mixed(expo_ref, chosen_ref, near + tile)
        return carry

    lax.fori_loop(0, chips, one_mix, 0, unroll=2)
    picked = jnp.zeros((dim, lanes), F32)
    for page in range(expo_ref.shape[0]):
        picked = jnp.where(iota((dim, lanes), 1) // 64 == page, chosen_ref[page, near + chip].astype(F32), picked)
    target_ref[...] = picked


def add_kernel(place_ref, keep_ref, total_ref, pair_ref, send_ref, own_ref):
    chips, dim, _ = keep_ref.shape
    total = total_ref[...] + joined_total(pair_ref[0, dim:dim + 16, 0:128], pair_ref[0, dim:dim + 16, 128:256])
    high, low = split_total(total)
    for tile in range(chips):
        send_ref[tile, 0:dim, :] = (keep_ref[tile] + pair_ref[tile, 0:dim, :].astype(F32)).astype(BF16)
        send_ref[tile, dim:dim + 16, 0:128] = high
        send_ref[tile, dim:dim + 16, 128:256] = low
    chip = place_ref[1]
    own_ref[...] = keep_ref[chip] + pair_ref[chip, 0:dim, :].astype(F32)


def gradient_kernel(multiplier, place_ref, index_ref, expo_ref, received_ref, own_ref, target_ref, near_ref, far_ref, page_raw,
                    hidden, query_raw_ref, query_hidden, give_ref, query_grad_ref, page_direction_ref, query_direction_ref,
                    inverse_total, score_grad, summed_grad):
    core, chip = place_ref[0], place_ref[1]
    chips, dim, lanes = near_ref.shape
    tiles = 2 * chips
    mine = core * chips + chip
    pages, slots, _ = hidden.shape
    parts = slots // 256
    total = jnp.zeros((tiles, 128), F32)
    for source in range(chips):
        total = total + joined_total(received_ref[source, dim:dim + 16, 0:128], received_ref[source, dim:dim + 16, 128:256])
    inverse = 1.0 / total
    first = iota((tiles, 128), 1) % 32 < 16
    inverse_total[:, 0:128] = jnp.where(first, inverse, pltpu.roll(inverse, 16, 1))
    inverse_total[:, 128:256] = jnp.where(first, pltpu.roll(inverse, 112, 1), inverse)
    half = give_ref.shape[0]
    columns = pl.ds(pl.multiple_of((1 - core) * half, half), half)

    def scattered(page, tile, weighted):
        index = index_ref[page, pl.ds(tile, 1), :]
        which = index >> 8
        left = jnp.concatenate([jnp.where(which == part, weighted, 0.0).astype(BF16) for part in range(parts)], axis=0)
        return lax.dot_general(left, one_hot(index & 255), NT, preferred_element_type=F32)

    for page in range(pages):
        is_target = (iota((tiles, lanes), 0) == mine) & (iota((tiles, lanes), 1) // 64 == page)
        score_grad[...] = (expo_ref[page] * inverse_total[...] - jnp.where(is_target, 1.0, 0.0)) * multiplier
        weighted = near_ref[chip].astype(F32) * score_grad[pl.ds(mine, 1), :]
        summed_grad[...] = scattered(page, mine, weighted - weighted.astype(BF16).astype(F32))
        for side, queries_ref in ((core, near_ref), (1 - core, far_ref)):
            for chip_of in range(chips):
                tile = side * chips + chip_of
                summed_grad[...] += scattered(page, tile, queries_ref[chip_of].astype(F32) * score_grad[pl.ds(tile, 1), :])
        grad = jnp.concatenate([summed_grad[part * dim:(part + 1) * dim] for part in range(parts)], axis=1)
        direction = unit_backward(grad, page_raw[page]).astype(BF16)
        page_direction_ref[page] = direction
    summed = own_ref[...]
    for source in range(chips):
        summed = summed + jnp.where(chip == source, 0.0, received_ref[source, 0:dim, :].astype(F32))
    query_grad = (summed * inverse_total[pl.ds(mine, 1), :] - target_ref[...]) * multiplier
    query_grad_ref[...] = query_grad.T
    direction = unit_backward(query_grad, query_raw_ref[...]).astype(BF16)
    query_direction_ref[...] = direction
    grad = jnp.dot(direction, query_hidden[:, columns], preferred_element_type=F32)
    for page in range(pages):
        grad = grad + jnp.dot(page_direction_ref[page], hidden[page, :, columns], preferred_element_type=F32)
    give_ref[...] = grad.T


def weight_keep_kernel(place_ref, page_direction_ref, query_direction_ref, hidden, query_hidden, keep_ref):
    half = keep_ref.shape[0]
    columns = pl.ds(pl.multiple_of(place_ref[0] * half, half), half)
    grad = jnp.dot(query_direction_ref[...], query_hidden[:, columns], preferred_element_type=F32)
    for page in range(hidden.shape[0]):
        grad = grad + jnp.dot(page_direction_ref[page], hidden[page, :, columns], preferred_element_type=F32)
    keep_ref[...] = grad.T


def shape(dims, kind):
    return jax.ShapeDtypeStruct(dims, kind)


def vmem(mib):
    return pltpu.CompilerParams(vmem_limit_bytes=mib * MIB)


def cost(flops, read):
    return pl.CostEstimate(flops=flops, bytes_accessed=read, transcendentals=0)


def swap_cores(value):
    return lax.ppermute(value, "core", [(0, 1), (1, 0)])


def summed(terms):
    return lax.optimization_barrier(jnp.sum(terms.astype(F32), axis=0)).astype(BF16)


def to_all(value, axis):
    return lax.all_to_all(jnp.broadcast_to(value[None], (lax.axis_size(axis),) + value.shape), axis, 0, 0, tiled=True)


def per_device(query_hidden, document_states, projection, lengths, best_token):
    query_count, tokens, hidden_size = query_hidden.shape
    pages, slots, _ = document_states.shape
    dim = projection.shape[1]
    chips, cores = lax.axis_size("chip"), lax.axis_size("core")
    tiles = chips * cores
    rows = query_count * tokens
    multiplier = 1.0 / (tokens * TEMPERATURE)
    smem = pl.BlockSpec(memory_space=pltpu.SMEM)
    inside = pl.BlockSpec(memory_space=pltpu.VMEM)
    anywhere = pl.BlockSpec(memory_space=pl.ANY)
    place = jnp.stack([lax.axis_index("core"), lax.axis_index("chip")]).astype(jnp.int32)
    query_rows = query_hidden.reshape(rows, hidden_size)

    query_raw, query_send = pl.pallas_call(
        query_kernel,
        in_specs=[anywhere] * 2,
        out_shape=(shape((dim, rows), F32), shape((chips, dim, rows), BF16)),
        scratch_shapes=[pltpu.VMEM((rows, hidden_size), BF16), pltpu.VMEM((hidden_size, dim), BF16), pltpu.SemaphoreType.DMA((2,))],
        compiler_params=vmem(QUERY_MIB),
        cost_estimate=cost(2 * rows * hidden_size * dim, 2 * MIB),
        name="query_project",
    )(query_rows, projection)
    near = lax.all_to_all(query_send, "chip", 0, 0, tiled=True)

    page_raw, page_unit, chosen, index = pl.pallas_call(
        page_kernel,
        in_specs=[anywhere] * 4,
        out_specs=[anywhere] * 4,
        out_shape=(
            shape((pages, dim, slots), F32),
            shape((pages, slots, dim), BF16),
            shape((pages, tiles, dim, rows), BF16),
            shape((pages, tiles, rows), jnp.int32),
        ),
        scratch_shapes=[
            pltpu.VMEM((pages, slots, hidden_size), BF16),
            pltpu.VMEM((hidden_size, dim), BF16),
            pltpu.VMEM((tokens, pages, chips * cores * query_count), jnp.int32),
            pltpu.SMEM((pages,), jnp.int32),
            pltpu.VMEM((128, 128), F32),
            pltpu.VMEM((pages, dim, slots), F32),
            pltpu.VMEM((pages, slots, dim), BF16),
            pltpu.VMEM((pages, tiles, dim, rows), BF16),
            pltpu.VMEM((pages, tiles, rows), jnp.int32),
            pltpu.SemaphoreType.DMA((pages + 4,)),
            pltpu.SemaphoreType.DMA((4, pages)),
            pltpu.SemaphoreType.DMA,
        ],
        compiler_params=vmem(PAGE_MIB),
        cost_estimate=cost(2 * pages * slots * dim * (hidden_size + tiles * rows), 16 * MIB),
        name="page_project",
    )(lengths, document_states, projection, jnp.transpose(best_token, (1, 2, 0)))

    near, index = lax.optimization_barrier((near, index))
    far = swap_cores(near)
    near_best, page_hidden = pl.pallas_call(
        near_kernel,
        in_specs=[inside] * 2 + [anywhere],
        out_shape=(shape((pages, chips, rows), F32), shape((pages, slots, hidden_size), BF16)),
        scratch_shapes=[pltpu.SemaphoreType.DMA],
        compiler_params=vmem(NEAR_MIB),
        cost_estimate=cost(pages * slots * dim * tiles * rows, 2 * MIB),
        name="near_scores",
    )(near, page_unit, document_states)
    expo, total, pair = pl.pallas_call(
        lambda *refs: far_kernel(multiplier, *refs),
        in_specs=[smem] + [inside] * 4,
        out_shape=(shape((pages, tiles, rows), F32), shape((tiles, 128), F32), shape((chips, dim + 16, rows), BF16)),
        scratch_shapes=[pltpu.VMEM((pages, tiles, rows), F32)],
        compiler_params=vmem(FAR_MIB),
        cost_estimate=cost(pages * slots * dim * tiles * rows, 8 * MIB),
        name="far_scores",
    )(place, far, page_unit, near_best, chosen)
    keep, target = pl.pallas_call(
        keep_kernel,
        in_specs=[smem] + [inside] * 2,
        out_shape=(shape((chips, dim, rows), F32), shape((dim, rows), F32)),
        compiler_params=vmem(24),
        cost_estimate=cost(2 * pages * dim * tiles * rows, 4 * MIB),
        name="keep_terms",
    )(place, expo, chosen)
    send, own = pl.pallas_call(
        add_kernel,
        in_specs=[smem] + [inside] * 3,
        out_shape=(shape((chips, dim + 16, rows), BF16), shape((dim, rows), F32)),
        compiler_params=vmem(8),
        name="add_pair",
    )(place, keep, total, swap_cores(pair))
    received = lax.all_to_all(send, "chip", 0, 0, tiled=True)

    half = hidden_size // cores
    weight_give, query_grad, page_direction, query_direction = pl.pallas_call(
        lambda *refs: gradient_kernel(multiplier, *refs),
        in_specs=[smem] + [inside] * 11,
        out_shape=(
            shape((half, dim), F32),
            shape((rows, dim), F32),
            shape((pages, dim, slots), BF16),
            shape((dim, rows), BF16),
        ),
        scratch_shapes=[
            pltpu.VMEM((tiles, rows), F32),
            pltpu.VMEM((tiles, rows), F32),
            pltpu.VMEM((slots // 256 * dim, 256), F32),
        ],
        compiler_params=vmem(GRADIENT_MIB),
        cost_estimate=cost(2 * pages * slots * dim * (hidden_size + tiles * rows), 16 * MIB),
        name="gradients",
    )(place, index, expo, received, own, target, near, far, page_raw, page_hidden, query_raw, query_rows)

    weight_keep = pl.pallas_call(
        weight_keep_kernel,
        in_specs=[smem] + [inside] * 4,
        out_shape=shape((half, dim), F32),
        compiler_params=vmem(GRADIENT_MIB),
        cost_estimate=cost(pages * slots * dim * hidden_size, 6 * MIB),
        name="weight_keep",
    )(place, page_direction, query_direction, page_hidden, query_rows)

    halves = (weight_keep + swap_cores(weight_give)).astype(BF16)
    chunk = summed(lax.all_to_all(halves.reshape(chips, half // chips, dim), "chip", 0, 0, tiled=True))
    chunk = summed(to_all(chunk, "dp"))
    mine = to_all(chunk, "chip").reshape(half, dim)
    other = swap_cores(mine)
    first = lax.axis_index("core") == 0
    weight_grad = jnp.concatenate([jnp.where(first, mine, other), jnp.where(first, other, mine)], axis=0).astype(F32)
    return (weight_grad, query_grad.reshape(query_count, tokens, dim))


def solution(mesh):
    groups, gallery = mesh.devices.shape
    levels = Mesh(mesh.devices.reshape(groups, gallery // 2, 2), ("dp", "chip", "core"))
    every = ("dp", "chip", "core")
    return jax.shard_map(
        per_device,
        mesh=levels,
        in_specs=(P(every, None, None), P(every, None, None), P(), P(every), P("dp", None, ("chip", "core"))),
        out_specs=(P(), P(every, None, None)),
        check_vma=False,
    )
```

```python
import jax
import jax.numpy as jnp
from jax import lax
from jax.experimental import pallas as pl
from jax.experimental.pallas import tpu as pltpu
from jax.sharding import Mesh, PartitionSpec as P

F32 = jnp.float32
BF16 = jnp.bfloat16
EPSILON = 1e-06
TEMPERATURE = 0.02
MIB = 1024 * 1024
QUERY_MIB, PAGE_MIB, NEAR_MIB, FAR_MIB, GRADIENT_MIB = 60, 56, 40, 24, 14

NT = (((1,), (1,)), ((), ()))


def inverse_norm(raw):
    value = jnp.sum(raw * raw, axis=0, keepdims=True) + EPSILON
    guess = lax.rsqrt(value)
    return guess * (1.5 - 0.5 * value * guess * guess)


def unit_backward(grad_unit, raw):
    inverse = inverse_norm(raw)
    unit = raw * inverse
    return (grad_unit - unit * jnp.sum(unit * grad_unit, axis=0, keepdims=True)) * inverse


def iota(shape, axis):
    return lax.broadcasted_iota(jnp.int32, shape, axis)


def one_hot(low):
    index = low.astype(F32).astype(BF16)
    positions = iota((256, low.shape[1]), 0).astype(F32).astype(BF16)
    return jnp.where(positions == index, jnp.ones((), BF16), jnp.zeros((), BF16))


def query_kernel(hidden_any, weight_any, raw_ref, send_ref, hidden, weight, arrived):
    copies = [
        pltpu.make_async_copy(weight_any, weight, arrived.at[0]),
        pltpu.make_async_copy(hidden_any, hidden, arrived.at[1]),
    ]
    for copy in copies:
        copy.start()
    for copy in copies:
        copy.wait()
    raw = jnp.dot(hidden[...], weight[...], preferred_element_type=F32).T
    raw_ref[...] = raw
    unit = (raw * inverse_norm(raw)).astype(BF16)
    for block in range(send_ref.shape[0]):
        send_ref[block] = unit


def page_kernel(length_any, hidden_any, weight_any, best_any, raw_any, unit_any, chosen_any, index_any,
                hidden, weight, best, length, turned, raw_ref, unit_ref, chosen_ref, index_ref, arrived, left, index_left):
    pages, slots, _ = hidden.shape
    dim, tiles = weight.shape[1], index_ref.shape[1]
    parts = slots // 256
    small = [
        pltpu.make_async_copy(best_any, best, arrived.at[pages]),
        pltpu.make_async_copy(weight_any, weight, arrived.at[pages + 1]),
        pltpu.make_async_copy(length_any, length, arrived.at[pages + 2]),
    ]

    def page_copy(page):
        return pltpu.make_async_copy(hidden_any.at[page], hidden.at[page], arrived.at[page])

    def first_copy(part):
        some = pl.ds(part * slots // 2, slots // 2)
        return pltpu.make_async_copy(hidden_any.at[0, some], hidden.at[0, some], arrived.at[pages + 2 + part if part else 0])

    def raw_copy(page):
        return pltpu.make_async_copy(raw_ref.at[page], raw_any.at[page], left.at[0, page])

    def unit_copy(page):
        return pltpu.make_async_copy(unit_ref.at[page], unit_any.at[page], left.at[1, page])

    def chosen_copy(page, part):
        some = pl.ds(part * (tiles // 2), tiles // 2)
        return pltpu.make_async_copy(chosen_ref.at[page, some], chosen_any.at[page, some], left.at[2 + part, page])

    first_copy(0).start()
    for copy in small:
        copy.start()
    first_copy(1).start()
    page_copy(1).start()
    small[0].wait()
    for page in range(pages):
        tokens = best[:, page, :].astype(F32)
        turned[...] = jnp.concatenate([tokens, jnp.zeros((96, 128), F32)], axis=0).T
        for core in range(2):
            halves = []
            for half in range(2):
                row = jnp.zeros((8, 128), F32)
                for query in range(4):
                    piece = turned[pl.ds(core * 8 + half * 4 + query, 8, stride=16), :]
                    row = row + (pltpu.roll(piece, 32 * query, 1) if query else piece)
                halves.append(row)
            index_ref[page, core * 8:core * 8 + 8, :] = jnp.concatenate(halves, axis=1).astype(jnp.int32)
    index_copy = pltpu.make_async_copy(index_ref, index_any, index_left)
    index_copy.start()
    small[1].wait()
    small[2].wait()

    def project(page):
        if page + 2 < pages:
            page_copy(page + 2).start()
        if page:
            page_copy(page).wait()
            raw_ref[page] = jnp.dot(hidden[page], weight[...], preferred_element_type=F32).T
        else:
            for part in range(2):
                some = slice(part * slots // 2, (part + 1) * slots // 2)
                first_copy(part).wait()
                raw_ref[0, :, some] = jnp.dot(hidden[0, some], weight[...], preferred_element_type=F32).T
        raw_copy(page).start()

    project(0)
    for page in range(pages):
        if page + 1 < pages:
            project(page + 1)
        raw = raw_ref[page]
        unit = raw * inverse_norm(raw)
        unit_ref[page] = jnp.where(iota(unit.shape, 1) < length[page], unit, unit[:, 0:1]).T.astype(BF16)
        unit_copy(page).start()
        unit = unit.astype(BF16)
        table = jnp.concatenate([unit[:, part * 256:(part + 1) * 256] for part in range(parts)], axis=0)

        for tile in range(tiles):
            index = index_ref[page, tile:tile + 1, :]
            found = jnp.dot(table, one_hot(index & 255), preferred_element_type=F32)
            which = index >> 8
            chosen = found[0:dim]
            for part in range(1, parts):
                chosen = jnp.where(which == part, found[part * dim:(part + 1) * dim], chosen)
            chosen_ref[page, tile] = chosen.astype(BF16)
            if (tile + 1) % (tiles // 2) == 0:
                chosen_copy(page, tile // (tiles // 2)).start()
    index_copy.wait()
    for page in range(pages):
        raw_copy(page).wait()
        unit_copy(page).wait()
        for part in range(2):
            chosen_copy(page, part).wait()


def best_scores(queries, unit_ref, out, row):
    for page in range(unit_ref.shape[0]):
        scores = jnp.dot(unit_ref[page], queries, preferred_element_type=F32)
        top = jnp.max(scores.reshape(-1, 8, scores.shape[1]), axis=0)
        out[page, pl.ds(row, 1), :] = jnp.max(top, axis=0, keepdims=True)


def near_kernel(query_ref, unit_ref, hidden_any, best_ref, hidden_ref, arrived):
    hidden_copy = pltpu.make_async_copy(hidden_any, hidden_ref, arrived)
    hidden_copy.start()

    for tile in range(query_ref.shape[0]):
        best_scores(query_ref[tile], unit_ref, best_ref, tile)
    hidden_copy.wait()


def split_total(total):
    high = total.astype(BF16)
    rest = total - high.astype(F32)
    middle = rest.astype(BF16).astype(F32)
    return high, jnp.where(iota(total.shape, 1) % 16 < 8, middle, rest - middle).astype(BF16)


def joined_total(high, small):
    small = small.astype(F32)
    other = jnp.where(iota(small.shape, 1) % 16 < 8, pltpu.roll(small, 120, 1), pltpu.roll(small, 8, 1))
    return high.astype(F32) + (small + other)


def mixed(expo_ref, chosen_ref, tile):
    result = expo_ref[0, pl.ds(tile, 1), :] * chosen_ref[0, tile].astype(F32)
    for page in range(1, expo_ref.shape[0]):
        result = result + expo_ref[page, pl.ds(tile, 1), :] * chosen_ref[page, tile].astype(F32)
    return result


def far_kernel(multiplier, place_ref, query_ref, unit_ref, near_ref, chosen_ref, expo_ref, total_ref, pair_ref, best):
    core = place_ref[0]
    pages, chips = near_ref.shape[:2]
    dim, lanes = query_ref.shape[1:]
    near = pl.multiple_of(core * chips, chips)
    far = pl.multiple_of((1 - core) * chips, chips)
    for page in range(pages):
        best[page, pl.ds(near, chips), :] = near_ref[page]

    for tile in range(chips):
        best_scores(query_ref[tile], unit_ref, best, far + tile)

    segment = jnp.where(iota((lanes, lanes), 0) // 32 == iota((lanes, lanes), 1) // 32, 1.0, 0.0).astype(BF16)
    value = best[...].reshape(pages * 2 * chips, lanes)
    score = jnp.zeros_like(value)
    for _ in range(3):
        part = value.astype(BF16)
        score = score + jnp.dot(part, segment, preferred_element_type=F32)
        value = value - part.astype(F32)
    expo = jnp.exp(score * multiplier).reshape(pages, 2 * chips, lanes)
    expo_ref[...] = expo
    total = jnp.sum(expo, axis=0)
    total = jnp.where(iota((2 * chips, 128), 1) % 32 < 16, total[:, :128], total[:, 128:])
    total_ref[...] = total
    high, low = split_total(total)

    def one_mix(tile, carry):
        pair_ref[tile, 0:dim, :] = mixed(expo_ref, chosen_ref, far + tile).astype(BF16)
        pair_ref[tile, dim:dim + 16, 0:128] = high
        pair_ref[tile, dim:dim + 16, 128:256] = low
        return carry

    lax.fori_loop(0, chips, one_mix, 0, unroll=2)


def keep_kernel(place_ref, expo_ref, chosen_ref, keep_ref, target_ref):
    core, chip = place_ref[0], place_ref[1]
    chips, dim, lanes = keep_ref.shape
    near = core * chips

    def one_mix(tile, carry):
        keep_ref[tile] = mixed(expo_ref, chosen_ref, near + tile)
        return carry

    lax.fori_loop(0, chips, one_mix, 0, unroll=2)
    picked = jnp.zeros((dim, lanes), F32)
    for page in range(expo_ref.shape[0]):
        picked = jnp.where(iota((dim, lanes), 1) // 64 == page, chosen_ref[page, near + chip].astype(F32), picked)
    target_ref[...] = picked


def add_kernel(place_ref, keep_ref, total_ref, pair_ref, send_ref, own_ref):
    chips, dim, _ = keep_ref.shape
    total = total_ref[...] + joined_total(pair_ref[0, dim:dim + 16, 0:128], pair_ref[0, dim:dim + 16, 128:256])
    high, low = split_total(total)
    for tile in range(chips):
        send_ref[tile, 0:dim, :] = (keep_ref[tile] + pair_ref[tile, 0:dim, :].astype(F32)).astype(BF16)
        send_ref[tile, dim:dim + 16, 0:128] = high
        send_ref[tile, dim:dim + 16, 128:256] = low
    chip = place_ref[1]
    own_ref[...] = keep_ref[chip] + pair_ref[chip, 0:dim, :].astype(F32)


def gradient_kernel(multiplier, place_ref, index_ref, expo_ref, received_ref, own_ref, target_ref, near_ref, far_ref, page_raw,
                    hidden, query_raw_ref, query_hidden, give_ref, query_grad_ref, page_direction_ref, query_direction_ref,
                    inverse_total, score_grad, summed_grad):
    core, chip = place_ref[0], place_ref[1]
    chips, dim, lanes = near_ref.shape
    tiles = 2 * chips
    mine = core * chips + chip
    pages, slots, _ = hidden.shape
    parts = slots // 256
    total = jnp.zeros((tiles, 128), F32)
    for source in range(chips):
        total = total + joined_total(received_ref[source, dim:dim + 16, 0:128], received_ref[source, dim:dim + 16, 128:256])
    inverse = 1.0 / total
    first = iota((tiles, 128), 1) % 32 < 16
    inverse_total[:, 0:128] = jnp.where(first, inverse, pltpu.roll(inverse, 16, 1))
    inverse_total[:, 128:256] = jnp.where(first, pltpu.roll(inverse, 112, 1), inverse)
    half = give_ref.shape[0]
    columns = pl.ds(pl.multiple_of((1 - core) * half, half), half)

    def scattered(page, tile, weighted):
        index = index_ref[page, pl.ds(tile, 1), :]
        which = index >> 8
        left = jnp.concatenate([jnp.where(which == part, weighted, 0.0).astype(BF16) for part in range(parts)], axis=0)
        return lax.dot_general(left, one_hot(index & 255), NT, preferred_element_type=F32)

    for page in range(pages):
        is_target = (iota((tiles, lanes), 0) == mine) & (iota((tiles, lanes), 1) // 64 == page)
        score_grad[...] = (expo_ref[page] * inverse_total[...] - jnp.where(is_target, 1.0, 0.0)) * multiplier
        weighted = near_ref[chip].astype(F32) * score_grad[pl.ds(mine, 1), :]
        summed_grad[...] = scattered(page, mine, weighted - weighted.astype(BF16).astype(F32))
        for side, queries_ref in ((core, near_ref), (1 - core, far_ref)):
            for chip_of in range(chips):
                tile = side * chips + chip_of
                summed_grad[...] += scattered(page, tile, queries_ref[chip_of].astype(F32) * score_grad[pl.ds(tile, 1), :])
        grad = jnp.concatenate([summed_grad[part * dim:(part + 1) * dim] for part in range(parts)], axis=1)
        direction = unit_backward(grad, page_raw[page]).astype(BF16)
        page_direction_ref[page] = direction
    summed = own_ref[...]
    for source in range(chips):
        summed = summed + jnp.where(chip == source, 0.0, received_ref[source, 0:dim, :].astype(F32))
    query_grad = (summed * inverse_total[pl.ds(mine, 1), :] - target_ref[...]) * multiplier
    query_grad_ref[...] = query_grad.T
    direction = unit_backward(query_grad, query_raw_ref[...]).astype(BF16)
    query_direction_ref[...] = direction
    grad = jnp.dot(direction, query_hidden[:, columns], preferred_element_type=F32)
    for page in range(pages):
        grad = grad + jnp.dot(page_direction_ref[page], hidden[page, :, columns], preferred_element_type=F32)
    give_ref[...] = grad.T


def weight_keep_kernel(place_ref, page_direction_ref, query_direction_ref, hidden, query_hidden, keep_ref):
    half = keep_ref.shape[0]
    columns = pl.ds(pl.multiple_of(place_ref[0] * half, half), half)
    grad = jnp.dot(query_direction_ref[...], query_hidden[:, columns], preferred_element_type=F32)
    for page in range(hidden.shape[0]):
        grad = grad + jnp.dot(page_direction_ref[page], hidden[page, :, columns], preferred_element_type=F32)
    keep_ref[...] = grad.T


def shape(dims, kind):
    return jax.ShapeDtypeStruct(dims, kind)


def vmem(mib):
    return pltpu.CompilerParams(vmem_limit_bytes=mib * MIB)


def cost(flops, read):
    return pl.CostEstimate(flops=flops, bytes_accessed=read, transcendentals=0)


def swap_cores(value):
    return lax.ppermute(value, "core", [(0, 1), (1, 0)])


def summed(terms):
    return lax.optimization_barrier(jnp.sum(terms.astype(F32), axis=0)).astype(BF16)


def to_all(value, axis):
    return lax.all_to_all(jnp.broadcast_to(value[None], (lax.axis_size(axis),) + value.shape), axis, 0, 0, tiled=True)


def per_device(query_hidden, document_states, projection, lengths, best_token):
    query_count, tokens, hidden_size = query_hidden.shape
    pages, slots, _ = document_states.shape
    dim = projection.shape[1]
    chips, cores = lax.axis_size("chip"), lax.axis_size("core")
    tiles = chips * cores
    rows = query_count * tokens
    multiplier = 1.0 / (tokens * TEMPERATURE)
    smem = pl.BlockSpec(memory_space=pltpu.SMEM)
    inside = pl.BlockSpec(memory_space=pltpu.VMEM)
    anywhere = pl.BlockSpec(memory_space=pl.ANY)
    place = jnp.stack([lax.axis_index("core"), lax.axis_index("chip")]).astype(jnp.int32)
    query_rows = query_hidden.reshape(rows, hidden_size)

    query_raw, query_send = pl.pallas_call(
        query_kernel,
        in_specs=[anywhere] * 2,
        out_shape=(shape((dim, rows), F32), shape((chips, dim, rows), BF16)),
        scratch_shapes=[pltpu.VMEM((rows, hidden_size), BF16), pltpu.VMEM((hidden_size, dim), BF16), pltpu.SemaphoreType.DMA((2,))],
        compiler_params=vmem(QUERY_MIB),
        cost_estimate=cost(2 * rows * hidden_size * dim, 2 * MIB),
        name="query_project",
    )(query_rows, projection)
    near = lax.all_to_all(query_send, "chip", 0, 0, tiled=True)

    page_raw, page_unit, chosen, index = pl.pallas_call(
        page_kernel,
        in_specs=[anywhere] * 4,
        out_specs=[anywhere] * 4,
        out_shape=(
            shape((pages, dim, slots), F32),
            shape((pages, slots, dim), BF16),
            shape((pages, tiles, dim, rows), BF16),
            shape((pages, tiles, rows), jnp.int32),
        ),
        scratch_shapes=[
            pltpu.VMEM((pages, slots, hidden_size), BF16),
            pltpu.VMEM((hidden_size, dim), BF16),
            pltpu.VMEM((tokens, pages, chips * cores * query_count), jnp.int32),
            pltpu.SMEM((pages,), jnp.int32),
            pltpu.VMEM((128, 128), F32),
            pltpu.VMEM((pages, dim, slots), F32),
            pltpu.VMEM((pages, slots, dim), BF16),
            pltpu.VMEM((pages, tiles, dim, rows), BF16),
            pltpu.VMEM((pages, tiles, rows), jnp.int32),
            pltpu.SemaphoreType.DMA((pages + 4,)),
            pltpu.SemaphoreType.DMA((4, pages)),
            pltpu.SemaphoreType.DMA,
        ],
        compiler_params=vmem(PAGE_MIB),
        cost_estimate=cost(2 * pages * slots * dim * (hidden_size + tiles * rows), 16 * MIB),
        name="page_project",
    )(lengths, document_states, projection, jnp.transpose(best_token, (1, 2, 0)))

    near, index = lax.optimization_barrier((near, index))
    far = swap_cores(near)
    near_best, page_hidden = pl.pallas_call(
        near_kernel,
        in_specs=[inside] * 2 + [anywhere],
        out_shape=(shape((pages, chips, rows), F32), shape((pages, slots, hidden_size), BF16)),
        scratch_shapes=[pltpu.SemaphoreType.DMA],
        compiler_params=vmem(NEAR_MIB),
        cost_estimate=cost(pages * slots * dim * tiles * rows, 2 * MIB),
        name="near_scores",
    )(near, page_unit, document_states)
    expo, total, pair = pl.pallas_call(
        lambda *refs: far_kernel(multiplier, *refs),
        in_specs=[smem] + [inside] * 4,
        out_shape=(shape((pages, tiles, rows), F32), shape((tiles, 128), F32), shape((chips, dim + 16, rows), BF16)),
        scratch_shapes=[pltpu.VMEM((pages, tiles, rows), F32)],
        compiler_params=vmem(FAR_MIB),
        cost_estimate=cost(pages * slots * dim * tiles * rows, 8 * MIB),
        name="far_scores",
    )(place, far, page_unit, near_best, chosen)
    keep, target = pl.pallas_call(
        keep_kernel,
        in_specs=[smem] + [inside] * 2,
        out_shape=(shape((chips, dim, rows), F32), shape((dim, rows), F32)),
        compiler_params=vmem(24),
        cost_estimate=cost(2 * pages * dim * tiles * rows, 4 * MIB),
        name="keep_terms",
    )(place, expo, chosen)
    send, own = pl.pallas_call(
        add_kernel,
        in_specs=[smem] + [inside] * 3,
        out_shape=(shape((chips, dim + 16, rows), BF16), shape((dim, rows), F32)),
        compiler_params=vmem(8),
        name="add_pair",
    )(place, keep, total, swap_cores(pair))
    received = lax.all_to_all(send, "chip", 0, 0, tiled=True)

    half = hidden_size // cores
    weight_give, query_grad, page_direction, query_direction = pl.pallas_call(
        lambda *refs: gradient_kernel(multiplier, *refs),
        in_specs=[smem] + [inside] * 11,
        out_shape=(
            shape((half, dim), F32),
            shape((rows, dim), F32),
            shape((pages, dim, slots), BF16),
            shape((dim, rows), BF16),
        ),
        scratch_shapes=[
            pltpu.VMEM((tiles, rows), F32),
            pltpu.VMEM((tiles, rows), F32),
            pltpu.VMEM((slots // 256 * dim, 256), F32),
        ],
        compiler_params=vmem(GRADIENT_MIB),
        cost_estimate=cost(2 * pages * slots * dim * (hidden_size + tiles * rows), 16 * MIB),
        name="gradients",
    )(place, index, expo, received, own, target, near, far, page_raw, page_hidden, query_raw, query_rows)

    weight_keep = pl.pallas_call(
        weight_keep_kernel,
        in_specs=[smem] + [inside] * 4,
        out_shape=shape((half, dim), F32),
        compiler_params=vmem(GRADIENT_MIB),
        cost_estimate=cost(pages * slots * dim * hidden_size, 6 * MIB),
        name="weight_keep",
    )(place, page_direction, query_direction, page_hidden, query_rows)

    halves = weight_keep + swap_cores(weight_give)
    chunk = jnp.sum(lax.all_to_all(halves.reshape(chips, half // chips, dim), "chip", 0, 0, tiled=True), axis=0)
    chunk = summed(to_all(chunk, "dp"))
    mine = to_all(chunk, "chip").reshape(half, dim)
    other = swap_cores(mine)
    first = lax.axis_index("core") == 0
    weight_grad = jnp.concatenate([jnp.where(first, mine, other), jnp.where(first, other, mine)], axis=0).astype(F32)
    return (weight_grad, query_grad.reshape(query_count, tokens, dim))


def solution(mesh):
    groups, gallery = mesh.devices.shape
    levels = Mesh(mesh.devices.reshape(groups, gallery // 2, 2), ("dp", "chip", "core"))
    every = ("dp", "chip", "core")
    return jax.shard_map(
        per_device,
        mesh=levels,
        in_specs=(P(every, None, None), P(every, None, None), P(), P(every), P("dp", None, ("chip", "core"))),
        out_specs=(P(), P(every, None, None)),
        check_vma=False,
    )
```
